128 devices in a mesh: shard: 2 (over x_lo), context: 16 (over z, y), tensor: 4 (over x_hi, core).
Axes of the slice: x: 4 (x_hi: 2, x_lo: 2; x = x_hi * 2 + x_lo), y: 4, z: 4, core: 2. Of those that a mesh axis runs over, the one named last changes fastest.
Arguments:
- tokens: bfloat16 [4096, 1024], P(('shard', 'context')), may hold values from -6 to 6
- segment_ids: int32 [4096], P('shard'), may hold values from 0 to 4, as said below
- w_qkv: bfloat16 [1, 1024, 3, 1024], P(None, 'shard', None, 'tensor'), may hold values from -0.1875 to 0.1875
- b_qv: bfloat16 [1, 2, 1024], P(None, None, 'tensor'), may hold values from -0.75 to 0.75
- w_out: bfloat16 [1, 1024, 1024], P(None, 'tensor', 'shard'), may hold values from -4 to 4
- w_up: bfloat16 [1, 1024, 4096], P(None, 'shard', 'tensor'), may hold values from -0.1875 to 0.1875
- b_up: bfloat16 [1, 4096], P(None, 'tensor'), may hold values from -6 to 6
- w_down: bfloat16 [1, 4096, 1024], P(None, 'tensor', 'shard'), may hold values from -0.09375 to 0.09375
- out_bias: bfloat16 [1, 2, 1024], replicated, may hold values from -6 to 6
- ln_gain: bfloat16 [1, 2, 1024], replicated, may hold values from 0.25 to 1.75
- ln_bias: bfloat16 [1, 2, 1024], replicated, may hold values from -6 to 6
- cotangent: float32 [4096, 1024], P(('shard', 'context')), may hold values from -6 to 6
Outputs:
- hidden_out: float32 [4096, 1024], P(('shard', 'context', 'tensor'))
- grad_tokens: float32 [4096, 1024], P(('shard', 'context', 'tensor'))
- grad_w_qkv: float32 [1, 1024, 3, 1024], P(None, 'shard', None, 'tensor')
- grad_w_out: float32 [1, 1024, 1024], P(None, 'tensor', 'shard')
- grad_w_up: float32 [1, 1024, 4096], P(None, 'shard', 'tensor')
- grad_w_down: float32 [1, 4096, 1024], P(None, 'tensor', 'shard')
- grad_b_qv: float32 [1, 2, 1024], P(None, None, 'tensor')
- grad_b_up: float32 [1, 4096], P(None, 'tensor')
- grad_out_bias: float32 [1, 2, 1024], P(None, None, 'tensor')
- grad_ln_gain: float32 [1, 2, 1024], P(None, None, 'tensor')
- grad_ln_bias: float32 [1, 2, 1024], P(None, None, 'tensor')
The draws below stay inside these ranges and needn't reach their ends.
Inputs may be any that keep to these rules, and one draw needn't show every extreme that they name: `segment_ids`: within each sequence the ids never fall; they begin at 0 and end at 4; one document starts in the first block of 128 tokens and ends in the last.
All inputs are finite; a program needn't handle non-finite values.
Results may differ from the reference program's by a relative error of at most 0.023.
Values may be sent and summed in bfloat16 or wider, within the bound.
No kernel may reach another device: no remote copies, remote signals or barrier semaphores. Data moves between devices by JAX's collectives and lax.ppermute only.
A program may use at most 64 MiB of HBM per device.

```python
import jax
import jax.numpy as jnp
from jax import lax

D = 1024
FF = 4096
HD = 64
LAYERS = 1
LEN = 2048
SEQS = 2
BLK = 128
TOKENS = 4096


def draw_segment_ids(key, part):
    key = jax.random.fold_in(key, 7)
    parts = jax.random.split(key, 4)
    half = BLK // 2
    shape = (SEQS, 1)
    first = jax.random.randint(parts[0], shape, 1, half)
    second = jax.random.randint(parts[1], shape, half, BLK)
    third = LEN - BLK + jax.random.randint(parts[2], shape, 1, half)
    fourth = LEN - half + jax.random.randint(parts[3], shape, 0, half)
    place = jnp.arange(LEN, dtype=jnp.int32)[None, :]
    ids = (place >= first).astype(jnp.int32) + (place >= second).astype(jnp.int32)
    ids = ids + (place >= third).astype(jnp.int32) + (place >= fourth).astype(jnp.int32)
    return ids.reshape(SEQS * LEN)


def block_levels(stream_key, extent, pieces, smallest, top_value):
    def one(dim, blocks):
        draws = jax.random.uniform(jax.random.fold_in(jax.random.fold_in(stream_key, 6), dim), (blocks,), jnp.float32, smallest / len(pieces), top_value / len(pieces))
        return jnp.repeat(jnp.exp(draws), extent[dim] // blocks).reshape((-1,) + (1,) * (len(extent) - dim - 1))

    factor_of = one(*pieces[0])
    for cut in pieces[1:]:
        factor_of = factor_of * one(*cut)
    return factor_of


def bell_draw(own_key, extent, scale, reach, cuts=(), held_as=jnp.bfloat16):
    values = jax.random.normal(own_key, extent, jnp.float32) * scale
    if len(cuts) > 0:
        values = block_levels(own_key, extent, cuts, -0.22, 0.18) * values
    return jnp.clip(values, min=-reach, max=reach).astype(held_as)


def setup_inputs(seed: int = 0) -> dict:
    key_list = jax.random.split(jax.random.key(seed), 13)
    return {
        "tokens": bell_draw(key_list[0], (TOKENS, D), 1.0, 6.0, ((0, 32),)),
        "segment_ids": draw_segment_ids(jax.random.fold_in(key_list[12], 71), 0),
        "w_qkv": bell_draw(key_list[2], (LAYERS, D, 3, D), D ** -0.5, 0.1875, ((1, 2), (3, 4))),
        "b_qv": bell_draw(key_list[3], (LAYERS, 2, D), 0.05, 0.75, ((2, 4),)),
        "w_out": bell_draw(key_list[4], (LAYERS, D, D), (max(1, D * 4 // LEN)) ** -0.5, 4.0, ((1, 4), (2, 2))),
        "w_up": bell_draw(key_list[5], (LAYERS, D, FF), D ** -0.5, 0.1875, ((1, 2), (2, 4))),
        "b_up": bell_draw(key_list[6], (LAYERS, FF), 0.5, 6.0, ((1, 4),)),
        "w_down": bell_draw(key_list[7], (LAYERS, FF, D), FF ** -0.5, 0.09375, ((1, 4), (2, 2))),
        "out_bias": bell_draw(key_list[8], (LAYERS, 2, D), 0.5, 6.0),
        "ln_gain": jnp.clip(1.0 + 0.15 * jax.random.normal(key_list[9], (LAYERS, 2, D), jnp.float32), 0.25, 1.75).astype(jnp.bfloat16),
        "ln_bias": bell_draw(key_list[10], (LAYERS, 2, D), 0.5, 6.0),
        "cotangent": bell_draw(key_list[11], (TOKENS, D), 1.0, 6.0, ((0, 32),), jnp.float32),
    }


EPSILON = 1e-05
NEGATIVE = -1e+30
ROOT_HALF = 0.7071067811865476
HIGHEST = lax.Precision.HIGHEST

@jax.custom_vjp
def low(v):
    return lax.optimization_barrier(v.astype(jnp.bfloat16)).astype(jnp.float32)

@jax.custom_vjp
def low_back(v):
    return v

def low_keep(v):
    return (low(v), None)

def low_pass(kept, grad):
    return (grad,)

def back_keep(v):
    return (v, None)

def back_low(kept, grad):
    return (low(grad),)
low.defvjp(low_keep, low_pass)
low_back.defvjp(back_keep, back_low)

def layer_norm(summed, gain, shift):
    centred = summed - lax.optimization_barrier(jnp.mean(summed, axis=-1, keepdims=True))
    factor = lax.rsqrt(lax.optimization_barrier(jnp.mean(centred * centred, axis=-1, keepdims=True)) + EPSILON)
    return centred * factor * gain + shift

def attention(queries, keys, values, ids):
    heads = D // HD

    def split(array):
        return array.reshape(SEQS, LEN, heads, HD).transpose(0, 2, 1, 3).reshape(SEQS * heads, LEN, HD)
    id_rows = jnp.broadcast_to(ids.reshape(SEQS, 1, LEN), (SEQS, heads, LEN)).reshape(SEQS * heads, LEN)

    def one_head(operands):
        query_h, key_h, value_h, row_ids = operands
        scores = low_back(jnp.dot(query_h, key_h.T, precision=HIGHEST) * HD ** (-0.5))
        scores = jnp.where(row_ids[:, None] == row_ids[None, :], scores, NEGATIVE)
        probs = jax.nn.softmax(scores, axis=-1)
        return jnp.dot(probs, value_h, precision=HIGHEST)
    result = lax.map(jax.checkpoint(one_head), (split(queries), split(keys), split(values), id_rows))
    return result.reshape(SEQS, heads, LEN, HD).transpose(0, 2, 1, 3).reshape(SEQS * LEN, D)

def reference(tokens, segment_ids, w_qkv, b_qv, w_out, w_up, b_up, w_down, out_bias, ln_gain, ln_bias, cotangent):

    def forward(hidden, weight_qkv, bias_qv, weight_out, weight_up, bias_up, weight_down, bias_out, gains, shifts):
        for layer in range(LAYERS):
            hidden_low = low(hidden)
            mixed = jnp.einsum('td,dcj->tcj', hidden_low, weight_qkv[layer], precision=HIGHEST)
            queries = low(low_back(mixed[:, 0] + bias_qv[layer, 0]))
            keys = low(low_back(mixed[:, 1]))
            values = low(low_back(mixed[:, 2] + bias_qv[layer, 1]))
            context = low(low_back(attention(queries, keys, values, segment_ids)))
            branch = low_back(jnp.dot(context, weight_out[layer], precision=HIGHEST) + bias_out[layer, 0])
            middle = layer_norm(hidden + branch, gains[layer, 0], shifts[layer, 0])
            before = low_back(jnp.dot(low(middle), weight_up[layer], precision=HIGHEST) + bias_up[layer])
            after = 0.5 * before * (1.0 + lax.erf(before * ROOT_HALF))
            second = low_back(jnp.dot(low(after), weight_down[layer], precision=HIGHEST) + bias_out[layer, 1])
            hidden = layer_norm(middle + second, gains[layer, 1], shifts[layer, 1])
        return hidden
    floats = [array.astype(jnp.float32) for array in (tokens, w_qkv, b_qv, w_out, w_up, b_up, w_down, out_bias, ln_gain, ln_bias)]
    output, pullback = jax.vjp(forward, *floats)
    grads = pullback(cotangent.astype(jnp.float32))
    return (output, grads[0], grads[1], grads[3], grads[4], grads[6], grads[2], grads[5], grads[7], grads[8], grads[9])
```

```python
import functools

import jax
import jax.numpy as jnp
from jax import lax
from jax.experimental import pallas as pl
from jax.experimental.pallas import tpu as pltpu
from jax.sharding import PartitionSpec as P

HD = 64
HEADS = 4
BLK = 128
LEN = 2048
D = 1024
HALF = 512
COLS = 256
UNITS = 1024
RING = 16
EPSILON = 1e-05
NEGATIVE = -1e30
ROOT_HALF = 0.7071067811865476
DENSITY = 0.3989422804014327
BF = jnp.bfloat16
F32 = jnp.float32

NN = (((1,), (0,)), ((), ()))
NT = (((1,), (1,)), ((), ()))
TN = (((0,), (0,)), ((), ()))


def mm(a, b, dims=NN):
    return lax.dot_general(a, b, dims, preferred_element_type=F32)


def call(kernel, outs, scalars, *args, scratch=(), vmem=40):
    specs = [pl.BlockSpec(memory_space=pltpu.SMEM)]
    specs += [pl.BlockSpec(memory_space=pltpu.VMEM)] * len(args)
    return pl.pallas_call(
        kernel,
        out_shape=[jax.ShapeDtypeStruct(shape, dtype) for shape, dtype in outs],
        in_specs=specs,
        out_specs=[pl.BlockSpec(memory_space=pltpu.VMEM)] * len(outs),
        scratch_shapes=list(scratch),
        compiler_params=pltpu.CompilerParams(vmem_limit_bytes=vmem << 20),
    )(scalars, *args)


def half_at(shard, own):
    return pl.ds(pl.multiple_of((shard if own else 1 - shard) * HALF, HALF), HALF)


def by_head(rows):
    lane = lax.broadcasted_iota(jnp.int32, rows.shape, 1) // HD
    return jnp.concatenate(
        [jnp.where(lane == head, rows, jnp.zeros_like(rows)) for head in range(HEADS)], axis=0
    )


def norm_rows(summed, gain, shift):
    centred = summed - jnp.mean(summed, axis=-1, keepdims=True)
    factor = lax.rsqrt(jnp.mean(centred * centred, axis=-1, keepdims=True) + EPSILON)
    normed = centred * factor
    return normed * gain + shift, normed, factor


def norm_back(incoming, normed, factor, gain):
    scaled = incoming * gain
    centre = jnp.mean(scaled, axis=-1, keepdims=True)
    along = jnp.mean(scaled * normed, axis=-1, keepdims=True)
    return factor * (scaled - centre - normed * along)


def split_rows(place, rows_ref, mine_ref, theirs_ref):
    core = place[2]
    for part in range(2):
        mine = pl.multiple_of(part * 64 + core * 32, 32)
        theirs = pl.multiple_of(part * 64 + (1 - core) * 32, 32)
        mine_ref[pl.ds(part * 32, 32), :] = rows_ref[pl.ds(mine, 32), :]
        theirs_ref[pl.ds(part * 32, 32), :] = rows_ref[pl.ds(theirs, 32), :].astype(BF)


def attend_kernel(
    place, x, w_own, w_oth, b_qv, id_q, id_k, wo_own, wo_oth,
    q_ref, k_ref, v_ref, o_ref, ob_ref, lse_ref, mine_ref, theirs_ref, part_ref,
):
    shard, block = place[0], place[1]
    biases = b_qv[...].astype(F32)

    @pl.loop(0, LEN // 256)
    def _(step):
        rows = pl.ds(pl.multiple_of(step * 256, 256), 256)
        x_own, x_oth = x[shard, rows, :], x[1 - shard, rows, :]
        k_ref[rows, :] = (mm(x_own, w_own[1]) + mm(x_oth, w_oth[1])).astype(BF)
        v_ref[rows, :] = (mm(x_own, w_own[2]) + mm(x_oth, w_oth[2]) + biases[1:2]).astype(BF)

    rows = pl.ds(pl.multiple_of(block * BLK, BLK), BLK)
    q = (mm(x[shard, rows, :], w_own[0]) + mm(x[1 - shard, rows, :], w_oth[0]) + biases[0:1]).astype(BF)
    q_ref[...] = q
    q_heads = by_head(q * BF(HD ** -0.5))
    allowed = id_q[...] == id_k[...]
    lane = lax.broadcasted_iota(jnp.int32, (BLK, COLS), 1) // HD
    out = jnp.zeros((BLK, COLS), F32)
    lse_ref[...] = jnp.zeros((1, HEADS * BLK), F32)
    for head in range(HEADS):
        scores = mm(q_heads[head * BLK : (head + 1) * BLK], k_ref[...], NT)
        scores = jnp.where(allowed, scores, NEGATIVE)
        highest = jnp.max(scores, axis=-1, keepdims=True)
        weights = jnp.exp(scores - highest)
        total = jnp.sum(weights, axis=-1, keepdims=True)
        mixed = mm(weights.astype(BF), v_ref[...]) / total
        out = jnp.where(lane == head, mixed, out)
        column = jnp.broadcast_to(highest + jnp.log(total), (BLK, BLK))
        lse_ref[:, head * BLK : (head + 1) * BLK] = column.T[0:1, :]
    o_ref[...] = out
    low = out.astype(BF)
    ob_ref[...] = low
    part_ref[:, half_at(shard, True)] = mm(low, wo_own[...])
    part_ref[:, half_at(shard, False)] = mm(low, wo_oth[...])
    split_rows(place, part_ref, mine_ref, theirs_ref)


def first_norm_kernel(place, tokens, chip, recv, extra, gain, shift, h_ref, n_ref, f_ref, hb_ref):
    core = place[2]
    for part in range(2):
        rows = pl.ds(part * 32, 32)
        here = tokens[pl.ds(pl.multiple_of(part * 64 + core * 32, 32), 32), :].astype(F32)
        summed = here + (chip[rows, :] + recv[rows, :].astype(F32) + extra[0:1, :].astype(F32))
        middle, normed, factor = norm_rows(
            summed, gain[0:1, :].astype(F32), shift[0:1, :].astype(F32)
        )
        h_ref[rows, :] = middle
        n_ref[rows, :] = normed
        f_ref[rows, :] = jnp.broadcast_to(factor, (32, 128))
        hb_ref[rows, :] = middle.astype(BF)


def up_down_kernel(
    place, hb, up_own, down_own, other, b_up, ub_ref, slope_ref, mine_ref, theirs_ref, part_ref
):
    shard, core = place[0], place[2]
    own, oth = hb[:, half_at(shard, True)], hb[:, half_at(shard, False)]
    for side in range(2):
        cols = pl.ds(side * HALF, HALF)
        weight = other[:, side * 32 : side * 32 + 32, :].reshape(HALF, HALF)
        before = mm(own, up_own[:, cols]) + mm(oth, weight) + b_up[:, cols].astype(F32)
        bell = 0.5 * (1.0 + lax.erf(before * ROOT_HALF))
        ub_ref[:, cols] = (before * bell).astype(BF)
        slope_ref[:, cols] = bell + before * DENSITY * jnp.exp(-0.5 * before * before)
    after = ub_ref[...]
    part_ref[:, half_at(shard, True)] = mm(after, down_own[...])
    part_ref[:, half_at(shard, False)] = mm(after, other[:, 64:128, :].reshape(UNITS, HALF))
    mine_ref[...] = part_ref[pl.ds(pl.multiple_of(core * 64, 64), 64), :]
    theirs_ref[...] = part_ref[pl.ds(pl.multiple_of((1 - core) * 64, 64), 64), :].astype(BF)


def second_norm_kernel(
    place, middle, chip, recv, extra, gain, shift, cot, out_ref, dx_ref, dz_ref, sums_ref, keep
):
    core, far = place[2], place[3]
    gains = gain[1:2, :].astype(F32)
    summed = middle[...] + (chip[...] + recv[...].astype(F32) + extra[1:2, :].astype(F32))
    hidden, normed, factor = norm_rows(summed, gains, shift[1:2, :].astype(F32))
    keep[...] = hidden
    out_ref[...] = keep[pl.ds(pl.multiple_of(far * 32, 32), 32), :]
    grad = jnp.concatenate(
        [cot[pl.ds(pl.multiple_of(part * 64 + core * 32, 32), 32), :] for part in range(2)], axis=0
    )
    back = norm_back(grad, normed, factor, gains)
    dx_ref[...] = back
    low = back.astype(BF)
    dz_ref[...] = low
    sums_ref[0:1, :] = jnp.sum(low.astype(F32), axis=0, keepdims=True)
    sums_ref[1:2, :] = jnp.sum(grad * normed, axis=0, keepdims=True)
    sums_ref[2:3, :] = jnp.sum(grad, axis=0, keepdims=True)
    sums_ref[3:8, :] = jnp.zeros((5, D), F32)


def down_up_kernel(
    place, dz, slope, up_own, down_own, other, da_ref, mine_ref, theirs_ref, part_ref
):
    shard, core = place[0], place[2]
    own, oth = dz[:, half_at(shard, True)], dz[:, half_at(shard, False)]
    after = mm(own, down_own[...], NT) + mm(oth, other[:, 64:128, :].reshape(UNITS, HALF), NT)
    da_ref[...] = (after * slope[...]).astype(BF)
    before = da_ref[...]
    part_ref[:, half_at(shard, True)] = mm(before, up_own[...], NT)
    part_ref[:, half_at(shard, False)] = mm(
        before[:, 0:HALF], other[:, 0:32, :].reshape(HALF, HALF), NT
    ) + mm(before[:, HALF:UNITS], other[:, 32:64, :].reshape(HALF, HALF), NT)
    mine_ref[...] = part_ref[pl.ds(pl.multiple_of(core * 64, 64), 64), :]
    theirs_ref[...] = part_ref[pl.ds(pl.multiple_of((1 - core) * 64, 64), 64), :].astype(BF)


def unit_grads_kernel(place, hb, da, ub, dz, pair_fwd, pair_bwd, out_ref):
    shard = place[0]
    rows = jnp.concatenate([hb[:, half_at(shard, True)], pair_fwd[:, 256:768]], axis=0)
    units = jnp.concatenate([da[...], pair_bwd[:, 512:1536]], axis=0)
    out_ref[0:512, :] = mm(rows, units, TN).astype(BF)
    total = jnp.sum(units.astype(F32), axis=0, keepdims=True)
    out_ref[1024:1040, :] = jnp.broadcast_to(total, (16, UNITS)).astype(BF)
    after = jnp.concatenate([ub[...], pair_fwd[:, 768:1792]], axis=0)
    grads = jnp.concatenate([dz[:, half_at(shard, True)], pair_bwd[:, 0:512]], axis=0)
    for side in range(2):
        cols = slice(side * HALF, side * HALF + HALF)
        out_ref[512:1024, cols] = mm(after[:, cols], grads, TN).astype(BF)


def first_back_kernel(
    place, dx, chip, recv, normed, factor, gain, sums_in, d_ref, low_ref, sums_ref
):
    grad = dx[...] + (chip[...] + recv[...].astype(F32))
    back = norm_back(grad, normed[...], factor[:, 0:1], gain[0:1, :].astype(F32))
    d_ref[...] = back
    low = back.astype(BF)
    low_ref[...] = low
    sums_ref[...] = sums_in[...]
    sums_ref[3:4, :] = jnp.sum(low.astype(F32), axis=0, keepdims=True)
    sums_ref[4:5, :] = jnp.sum(grad * normed[...], axis=0, keepdims=True)
    sums_ref[5:6, :] = jnp.sum(grad, axis=0, keepdims=True)


def attend_back_kernel(
    place, q, k, v, o, lse, low, wo_own, wo_oth, id_q, id_k, dq_ref, dkv_ref, nat_ref, acc_ref
):
    shard = place[0]
    nat_ref[0:32, :] = low[0, 0:32, :]
    nat_ref[32:64, :] = low[1, 0:32, :]
    nat_ref[64:96, :] = low[0, 32:64, :]
    nat_ref[96:128, :] = low[1, 32:64, :]
    d_out = (
        mm(nat_ref[:, half_at(shard, True)], wo_own[...], NT)
        + mm(nat_ref[:, half_at(shard, False)], wo_oth[...], NT)
    ).astype(BF)
    turned = (d_out.astype(F32) * o[...]).T
    delta = jnp.concatenate(
        [
            jnp.sum(turned[head * HD : (head + 1) * HD], axis=0, keepdims=True)
            for head in range(HEADS)
        ],
        axis=1,
    )
    q_heads = by_head(q[...] * BF(HD ** -0.5))
    d_heads = by_head(d_out)
    acc_ref[...] = jnp.zeros_like(acc_ref)

    @pl.loop(0, LEN // 256)
    def _(step):
        rows = pl.ds(pl.multiple_of(step * 256, 256), 256)
        keys, values = k[rows, :], v[rows, :]
        allowed = id_k[rows, :] == id_q[...]
        probs = jnp.where(allowed, jnp.exp(mm(keys, q_heads, NT) - lse[...]), 0.0)
        d_scores = (probs * (mm(values, d_heads, NT) - delta)).astype(BF)
        dkv_ref[rows, 0:COLS] = mm(d_scores, q_heads).astype(BF)
        dkv_ref[rows, COLS : 2 * COLS] = mm(probs.astype(BF), d_heads).astype(BF)
        acc_ref[...] += mm(d_scores, keys, TN)

    lane = lax.broadcasted_iota(jnp.int32, (BLK, COLS), 1) // HD
    total = jnp.zeros((BLK, COLS), F32)
    for head in range(HEADS):
        total = jnp.where(lane == head, acc_ref[head * BLK : (head + 1) * BLK, :], total)
    dq_ref[...] = (total * HD ** -0.5).astype(BF)


def token_grad_kernel(place, dq, recv, w_own, w_oth, d_ref, mine_ref, theirs_ref, part_ref):
    shard = place[0]
    total = recv[0].astype(F32)
    for index in range(1, RING):
        total = total + recv[index].astype(F32)
    d_ref[:, 0:COLS] = dq[...]
    d_ref[:, COLS : 3 * COLS] = total.astype(BF)
    for own, weight in ((True, w_own), (False, w_oth)):
        part_ref[:, half_at(shard, own)] = (
            mm(d_ref[:, 0:COLS], weight[0], NT)
            + mm(d_ref[:, COLS : 2 * COLS], weight[1], NT)
            + mm(d_ref[:, 2 * COLS : 3 * COLS], weight[2], NT)
        )
    split_rows(place, part_ref, mine_ref, theirs_ref)


def in_grads_kernel(place, tokens, d, d_pair, pair_fwd, ob, low, low_pair, sums, out_ref):
    shard = place[0]
    rows = jnp.concatenate([tokens[:, half_at(shard, True)], pair_fwd[:, 1792:2304]], axis=0)
    grads = jnp.concatenate([d[...], d_pair[...]], axis=0)
    for part in range(3):
        term = mm(rows, grads[:, part * COLS : (part + 1) * COLS], TN).astype(BF)
        out_ref[:, part * 32 : part * 32 + 32, :] = term.reshape(RING, 32, COLS)
    heads = jnp.concatenate([ob[...], pair_fwd[:, 0:256]], axis=0)
    outs = jnp.concatenate([low[...], low_pair[...]], axis=0)
    for side in range(2):
        term = mm(heads, outs[:, side * COLS : (side + 1) * COLS], TN).astype(BF)
        out_ref[:, 96 + side * 16 : 112 + side * 16, :] = term.reshape(RING, 16, COLS)
    wide = grads.astype(F32)
    small = jnp.concatenate(
        [
            sums[0:6, :],
            jnp.sum(wide[:, 0:COLS], axis=0, keepdims=True),
            jnp.sum(wide[:, 2 * COLS : 3 * COLS], axis=0, keepdims=True),
            jnp.zeros((8, COLS), F32),
        ],
        axis=0,
    ).astype(BF)
    for index in range(RING):
        out_ref[index, 128:144, :] = small


def total_kernel(place, recv, small_ref, out_ref):
    total = recv[0].astype(F32)
    for index in range(1, RING):
        total = total + recv[index].astype(F32)
    small_ref[...] = total[128:144]
    low = total[0:128].astype(BF)
    for index in range(RING):
        out_ref[index] = low


def unpack_kernel(place, recv, in_ref, out_ref):
    for part in range(3):
        in_ref[part] = recv[:, part * 32 : part * 32 + 32, :].reshape(HALF, COLS).astype(F32)
    for side in range(2):
        out_ref[:, side * COLS : (side + 1) * COLS] = (
            recv[:, 96 + side * 16 : 112 + side * 16, :].reshape(COLS, COLS).astype(F32)
        )


def swap(value, axis, bit):
    size = lax.axis_size(axis)
    return lax.ppermute(value, axis, [(index, index ^ bit) for index in range(size)])


def pair_gather(value):
    return lax.all_gather(value, "tensor", axis=0, axis_index_groups=[[0, 1], [2, 3]])


def tensor_sum(mine, theirs):
    chip = mine + swap(theirs, "tensor", 1).astype(F32)
    return chip, swap(chip.astype(BF), "tensor", 2)


def shards(
    tokens, segment_ids, w_qkv, b_qv, w_out, w_up, b_up, w_down, out_bias, ln_gain, ln_bias, cotangent
):
    shard, block, tensor = (lax.axis_index(name) for name in ("shard", "context", "tensor"))
    core, far = tensor % 2, tensor // 2
    place = jnp.stack([shard, block, core, far]).astype(jnp.int32)
    w_in = jnp.transpose(w_qkv[0], (1, 0, 2))
    w_out, w_up, w_down = w_out[0], w_up[0], w_down[0]
    extra, gain, shift = out_bias[0], ln_gain[0], ln_bias[0]

    in_oth = swap(w_in, "shard", 1)
    out_oth = swap(w_out, "shard", 1)
    up_rows = lax.dynamic_slice_in_dim(w_up, block * 32, 32, 0)
    down_rows = lax.dynamic_slice_in_dim(w_down, block * 64, 64, 0)
    packed = jnp.concatenate([up_rows[:, :HALF], up_rows[:, HALF:], down_rows], axis=0)
    ff_oth = lax.all_gather(swap(packed, "shard", 1), "context", axis=0)

    mine = lax.dynamic_slice_in_dim(tokens, core * HALF, HALF, 1)
    spread = lax.all_to_all(
        jnp.broadcast_to(mine[None], (RING, BLK, HALF)), "context", 0, 0, tiled=True
    )
    x = pair_gather(spread.reshape(LEN, HALF))

    id_q = lax.dynamic_slice_in_dim(segment_ids, block * BLK, BLK, 0)
    q, k, v, o, ob, lse, mine, theirs = call(
        attend_kernel,
        [
            ((BLK, COLS), BF), ((LEN, COLS), BF), ((LEN, COLS), BF), ((BLK, COLS), F32),
            ((BLK, COLS), BF), ((1, HEADS * BLK), F32), ((64, D), F32), ((64, D), BF),
        ],
        place, x, w_in, in_oth, b_qv[0], id_q[:, None], segment_ids[None, :], w_out, out_oth,
        scratch=[pltpu.VMEM((BLK, D), F32)], vmem=48,
    )
    chip, recv = tensor_sum(mine, theirs)
    middle, normed, factor, low_mid = call(
        first_norm_kernel,
        [((64, D), F32), ((64, D), F32), ((64, 128), F32), ((64, D), BF)],
        place, tokens, chip, recv, extra, gain, shift,
    )
    hb = pair_gather(low_mid).reshape(BLK, D)
    ub, slope, mine, theirs = call(
        up_down_kernel,
        [((BLK, UNITS), BF), ((BLK, UNITS), F32), ((64, D), F32), ((64, D), BF)],
        place, hb, w_up, w_down, ff_oth, b_up,
        scratch=[pltpu.VMEM((BLK, D), F32)],
    )
    away = (1 - shard) * HALF
    pair_fwd = swap(
        jnp.concatenate(
            [
                ob,
                lax.dynamic_slice_in_dim(hb, away, HALF, 1),
                ub,
                lax.dynamic_slice_in_dim(tokens, away, HALF, 1),
            ],
            axis=1,
        ),
        "shard", 1,
    )
    chip, recv = tensor_sum(mine, theirs)
    hidden_out, dx, low_second, sums = call(
        second_norm_kernel,
        [((32, D), F32), ((64, D), F32), ((64, D), BF), ((8, D), F32)],
        place, middle, chip, recv, extra, gain, shift, cotangent,
        scratch=[pltpu.VMEM((64, D), F32)],
    )
    dz = pair_gather(low_second).reshape(BLK, D)
    da, mine, theirs = call(
        down_up_kernel,
        [((BLK, UNITS), BF), ((64, D), F32), ((64, D), BF)],
        place, dz, slope, w_up, w_down, ff_oth,
        scratch=[pltpu.VMEM((BLK, D), F32)],
    )
    pair_bwd = swap(
        jnp.concatenate([lax.dynamic_slice_in_dim(dz, away, HALF, 1), da], axis=1), "shard", 1
    )
    chip, recv = tensor_sum(mine, theirs)
    (unit_grads,) = call(
        unit_grads_kernel, [((1040, UNITS), BF)], place, hb, da, ub, dz, pair_fwd, pair_bwd
    )
    unit_total = lax.psum(unit_grads, "context")
    d_first, low_first, sums = call(
        first_back_kernel,
        [((64, D), F32), ((64, D), BF), ((8, D), F32)],
        place, dx, chip, recv, normed, factor, gain, sums,
    )
    low_pairs = pair_gather(low_first)
    dq, dkv = call(
        attend_back_kernel,
        [((BLK, COLS), BF), ((LEN, 2 * COLS), BF)],
        place, q, k, v, o, lse, low_pairs, w_out, out_oth,
        jnp.tile(id_q[None, :], (1, HEADS)), segment_ids[:, None],
        scratch=[pltpu.VMEM((BLK, D), BF), pltpu.VMEM((HEADS * BLK, COLS), F32)], vmem=48,
    )
    sums = sums + swap(sums, "tensor", 1)
    sums = lax.dynamic_slice_in_dim(sums, tensor * COLS, COLS, 1)
    sums = sums + swap(sums, "shard", 1)
    low_rows = low_pairs.reshape(2, 2, 32, D).transpose(1, 0, 2, 3).reshape(BLK, D)
    low_pair = swap(lax.dynamic_slice_in_dim(low_rows, away, HALF, 1), "shard", 1)
    low_own = lax.dynamic_slice_in_dim(low_rows, shard * HALF, HALF, 1)
    recv = lax.all_to_all(dkv, "context", 0, 0, tiled=True).reshape(RING, BLK, 2 * COLS)
    d_mixed, mine, theirs = call(
        token_grad_kernel,
        [((BLK, 3 * COLS), BF), ((64, D), F32), ((64, D), BF)],
        place, dq, recv, w_in, in_oth,
        scratch=[pltpu.VMEM((BLK, D), F32)],
    )
    d_pair = swap(d_mixed, "shard", 1)
    chip = mine + swap(theirs, "tensor", 1).astype(F32)
    chip_far = lax.dynamic_slice_in_dim(chip, (1 - far) * 32, 32, 0).astype(BF)
    grad_tokens = (
        lax.dynamic_slice_in_dim(d_first + chip, far * 32, 32, 0)
        + swap(chip_far, "tensor", 2).astype(F32)
    )
    (in_grads,) = call(
        in_grads_kernel, [((RING, 144, COLS), BF)],
        place, tokens, d_mixed, d_pair, pair_fwd, ob, low_own, low_pair, sums,
    )
    recv = lax.all_to_all(in_grads, "context", 0, 0, tiled=True)
    small, totals = call(
        total_kernel, [((16, COLS), F32), ((RING, 128, COLS), BF)], place, recv
    )
    recv = lax.all_to_all(totals, "context", 0, 0, tiled=True)
    grad_in, grad_w_out = call(
        unpack_kernel, [((3, HALF, COLS), F32), ((COLS, HALF), F32)], place, recv
    )
    unit_total = unit_total.astype(F32)
    grad_w_down = jnp.concatenate([unit_total[512:1024, :HALF], unit_total[512:1024, HALF:]], axis=0)
    return (
        hidden_out,
        grad_tokens,
        jnp.transpose(grad_in, (1, 0, 2))[None],
        grad_w_out[None],
        unit_total[0:512][None],
        grad_w_down[None],
        small[6:8][None],
        unit_total[1024:1025],
        jnp.stack([small[3], small[0]])[None],
        jnp.stack([small[4], small[1]])[None],
        jnp.stack([small[5], small[2]])[None],
    )


def solution(mesh):
    rows = P(("shard", "context"), None)
    own_rows = P(("shard", "context", "tensor"), None)
    by_column = P(None, None, "tensor")
    in_specs = (
        rows,
        P("shard"),
        P(None, "shard", None, "tensor"),
        by_column,
        P(None, "tensor", "shard"),
        P(None, "shard", "tensor"),
        P(None, "tensor"),
        P(None, "tensor", "shard"),
        P(),
        P(),
        P(),
        rows,
    )
    out_specs = (
        own_rows,
        own_rows,
        P(None, "shard", None, "tensor"),
        P(None, "tensor", "shard"),
        P(None, "shard", "tensor"),
        P(None, "tensor", "shard"),
        by_column,
        P(None, "tensor"),
        by_column,
        by_column,
        by_column,
    )
    return jax.shard_map(shards, mesh=mesh, in_specs=in_specs, out_specs=out_specs, check_vma=False)
```

```python
import functools

import jax
import jax.numpy as jnp
from jax import lax
from jax.experimental import pallas as pl
from jax.experimental.pallas import tpu as pltpu
from jax.sharding import PartitionSpec as P

HD = 64
HEADS = 4
BLK = 128
LEN = 2048
D = 1024
HALF = 512
COLS = 256
UNITS = 1024
RING = 16
EPSILON = 1e-05
NEGATIVE = -1e30
ROOT_HALF = 0.7071067811865476
DENSITY = 0.3989422804014327
BF = jnp.bfloat16
F32 = jnp.float32

NN = (((1,), (0,)), ((), ()))
NT = (((1,), (1,)), ((), ()))
TN = (((0,), (0,)), ((), ()))


def mm(a, b, dims=NN):
    return lax.dot_general(a, b, dims, preferred_element_type=F32)


def call(kernel, micros, outs, scalars, *args, scratch=(), vmem=20):
    specs = [pl.BlockSpec(memory_space=pltpu.SMEM)]
    specs += [pl.BlockSpec(memory_space=pltpu.VMEM)] * len(args)
    return pl.pallas_call(
        kernel,
        out_shape=[jax.ShapeDtypeStruct(shape, dtype) for shape, dtype in outs],
        in_specs=specs,
        out_specs=[pl.BlockSpec(memory_space=pltpu.VMEM)] * len(outs),
        scratch_shapes=list(scratch),
        compiler_params=pltpu.CompilerParams(vmem_limit_bytes=vmem << 20),
        cost_estimate=pl.CostEstimate(
            flops=int(micros * 1.1e9), bytes_accessed=int(micros * 3e6), transcendentals=0
        ),
    )(scalars, *args)


def half_at(shard, own):
    return pl.ds(pl.multiple_of((shard if own else 1 - shard) * HALF, HALF), HALF)


def by_head(rows):
    lane = lax.broadcasted_iota(jnp.int32, rows.shape, 1) // HD
    return jnp.concatenate(
        [jnp.where(lane == head, rows, jnp.zeros_like(rows)) for head in range(HEADS)], axis=0
    )


def norm_rows(summed, gain, shift):
    centred = summed - jnp.mean(summed, axis=-1, keepdims=True)
    factor = lax.rsqrt(jnp.mean(centred * centred, axis=-1, keepdims=True) + EPSILON)
    normed = centred * factor
    return normed * gain + shift, normed, factor


def norm_back(incoming, normed, factor, gain):
    scaled = incoming * gain
    centre = jnp.mean(scaled, axis=-1, keepdims=True)
    along = jnp.mean(scaled * normed, axis=-1, keepdims=True)
    return factor * (scaled - centre - normed * along)


def split_rows(place, rows_ref, mine_ref, theirs_ref):
    core = place[2]
    for part in range(2):
        mine = pl.multiple_of(part * 64 + core * 32, 32)
        theirs = pl.multiple_of(part * 64 + (1 - core) * 32, 32)
        mine_ref[pl.ds(part * 32, 32), :] = rows_ref[pl.ds(mine, 32), :].astype(BF)
        theirs_ref[pl.ds(part * 32, 32), :] = rows_ref[pl.ds(theirs, 32), :].astype(BF)


def split_halves(place, rows_ref, mine_ref, theirs_ref):
    core = place[2]
    mine_ref[...] = rows_ref[pl.ds(pl.multiple_of(core * 64, 64), 64), :].astype(BF)
    theirs_ref[...] = rows_ref[pl.ds(pl.multiple_of((1 - core) * 64, 64), 64), :].astype(BF)


def core_rows(place, ref):
    core = place[2]
    return jnp.concatenate(
        [ref[pl.ds(pl.multiple_of(part * 64 + core * 32, 32), 32), :] for part in range(2)], axis=0
    )


def attend_kernel(
    place, x_mine, x_sib, w_own, w_oth, b_qv, id_q, id_k, wo_own, wo_oth,
    q_ref, k_ref, v_ref, o_ref, ob_ref, lse_ref, mine_ref, theirs_ref, part_ref,
):
    shard, block, core = place[0], place[1], place[2]
    biases = b_qv[...].astype(F32)
    own, oth = half_at(shard, True), half_at(shard, False)

    @pl.loop(0, RING // 4)
    def _(step):
        blocks = pl.ds(step * 4, 4)
        for x, side in ((x_mine, core), (x_sib, 1 - core)):
            x_own = x[blocks, :, own].reshape(256, HALF)
            x_oth = x[blocks, :, oth].reshape(256, HALF)
            queries = mm(x_own, w_own[0]) + mm(x_oth, w_oth[0]) + biases[0:1]
            keys = mm(x_own, w_own[1]) + mm(x_oth, w_oth[1])
            values = mm(x_own, w_own[2]) + mm(x_oth, w_oth[2]) + biases[1:2]
            q_ref[blocks, side] = queries.astype(BF).reshape(4, 64, COLS)
            k_ref[blocks, side] = keys.astype(BF).reshape(4, 64, COLS)
            v_ref[blocks, side] = values.astype(BF).reshape(4, 64, COLS)

    keys, values = k_ref[...].reshape(LEN, COLS), v_ref[...].reshape(LEN, COLS)
    q_heads = by_head(q_ref[block].reshape(BLK, COLS) * BF(HD ** -0.5))
    allowed = id_q[...] == id_k[...]
    lane = lax.broadcasted_iota(jnp.int32, (BLK, COLS), 1) // HD
    out = jnp.zeros((BLK, COLS), F32)
    for head in range(HEADS):
        scores = mm(q_heads[head * BLK : (head + 1) * BLK], keys, NT)
        scores = jnp.where(allowed, scores, NEGATIVE)
        highest = jnp.max(scores, axis=-1, keepdims=True)
        weights = jnp.exp(scores - highest)
        total = jnp.sum(weights, axis=-1, keepdims=True)
        mixed = mm(weights.astype(BF), values) / total
        out = jnp.where(lane == head, mixed, out)
        column = jnp.broadcast_to(highest + jnp.log(total), (BLK, BLK))
        lse_ref[:, head * BLK : (head + 1) * BLK] = column.T[0:1, :]
    o_ref[...] = out
    low = out.astype(BF)
    ob_ref[...] = low
    part_ref[:, own] = mm(low, wo_own[...])
    part_ref[:, oth] = mm(low, wo_oth[...])
    split_rows(place, part_ref, mine_ref, theirs_ref)


def first_norm(summed, gain, shift):
    return norm_rows(summed[...], gain[0:1, :].astype(F32), shift[0:1, :].astype(F32))


def first_norm_kernel(place, tokens, chip, recv, extra, gain, shift, s_ref, hb_ref):
    branch = chip[...].astype(F32) + recv[...].astype(F32) + extra[0:1, :].astype(F32)
    s_ref[...] = core_rows(place, tokens).astype(F32) + branch
    hb_ref[...] = first_norm(s_ref, gain, shift)[0].astype(BF)


def other_up(other, side):
    return other[:, side * 32 : side * 32 + 32, :].reshape(HALF, HALF)


def other_down(other):
    return other[:, 64:128, :].reshape(UNITS, HALF)


def up_down_kernel(
    place, hb, up_own, down_own, other, b_up,
    ub_ref, slope_ref, mine_ref, theirs_ref, part_ref,
):
    shard = place[0]
    own, oth = hb[:, half_at(shard, True)], hb[:, half_at(shard, False)]
    for side in range(2):
        cols = pl.ds(side * HALF, HALF)
        before = mm(own, up_own[:, cols]) + mm(oth, other_up(other, side)) + b_up[:, cols].astype(F32)
        bell = 0.5 * (1.0 + lax.erf(before * ROOT_HALF))
        ub_ref[:, cols] = (before * bell).astype(BF)
        slope_ref[:, cols] = bell + before * DENSITY * jnp.exp(-0.5 * before * before)
    after = ub_ref[...]
    part_ref[:, half_at(shard, True)] = mm(after, down_own[...])
    part_ref[:, half_at(shard, False)] = mm(after, other_down(other))
    split_halves(place, part_ref, mine_ref, theirs_ref)


def second_norm_kernel(
    place, first, chip, recv, extra, gain, shift, cot, out_ref, dx_ref, dz_ref, sums_ref, keep
):
    far = place[3]
    middle = first_norm(first, gain, shift)[0]
    gains = gain[1:2, :].astype(F32)
    branch = chip[...].astype(F32) + recv[...].astype(F32) + extra[1:2, :].astype(F32)
    hidden, normed, factor = norm_rows(middle + branch, gains, shift[1:2, :].astype(F32))
    keep[...] = hidden
    out_ref[...] = keep[pl.ds(pl.multiple_of(far * 32, 32), 32), :]
    grad = core_rows(place, cot)
    back = norm_back(grad, normed, factor, gains)
    dx_ref[...] = back
    low = back.astype(BF)
    dz_ref[...] = low
    sums_ref[0:1, :] = jnp.sum(low.astype(F32), axis=0, keepdims=True)
    sums_ref[1:2, :] = jnp.sum(grad * normed, axis=0, keepdims=True)
    sums_ref[2:3, :] = jnp.sum(grad, axis=0, keepdims=True)
    sums_ref[3:8, :] = jnp.zeros((5, D), F32)


def down_up_kernel(
    place, dz, slope, up_own, down_own, other, da_ref, mine_ref, theirs_ref, part_ref
):
    shard = place[0]
    own, oth = dz[:, half_at(shard, True)], dz[:, half_at(shard, False)]
    after = mm(own, down_own[...], NT) + mm(oth, other_down(other), NT)
    da_ref[...] = (after * slope[...]).astype(BF)
    before = da_ref[...]
    part_ref[:, half_at(shard, True)] = mm(before, up_own[...], NT)
    part_ref[:, half_at(shard, False)] = sum(
        mm(before[:, side * HALF : (side + 1) * HALF], other_up(other, side), NT) for side in range(2)
    )
    split_halves(place, part_ref, mine_ref, theirs_ref)


def unit_grads_kernel(place, hb, da, ub, dz, pair_fwd, pair_dz, pair_da, out_ref):
    shard = place[0]
    rows = jnp.concatenate([hb[:, half_at(shard, True)], pair_fwd[:, 0:512]], axis=0)
    units = jnp.concatenate([da[...], pair_da[...]], axis=0)
    after = jnp.concatenate([ub[...], pair_fwd[:, 512:1536]], axis=0)
    grads = jnp.concatenate([dz[:, half_at(shard, True)], pair_dz[...]], axis=0)
    for part in range(4):
        cols = slice(part * COLS, (part + 1) * COLS)
        term = mm(rows, units[:, cols], TN).astype(BF)
        out_ref[:, part * 32 : part * 32 + 32, :] = term.reshape(RING, 32, COLS)
    for side in range(2):
        cols = slice(side * COLS, (side + 1) * COLS)
        term = mm(after, grads[:, cols], TN).astype(BF)
        out_ref[:, 128 + side * 64 : 192 + side * 64, :] = term.reshape(RING, 64, COLS)
    total = jnp.sum(units.astype(F32), axis=0, keepdims=True)
    small = jnp.concatenate(
        [total[:, part * COLS : (part + 1) * COLS] for part in range(4)]
        + [jnp.zeros((12, COLS), F32)],
        axis=0,
    ).astype(BF)
    for index in range(RING):
        out_ref[index, 256:272, :] = small


def first_back_kernel(
    place, first, dx, chip, recv, gain, shift, sums_in, d_ref, low_ref, sums_ref, keep
):
    far = place[3]
    _, normed, factor = first_norm(first, gain, shift)
    grad = dx[...] + (chip[...].astype(F32) + recv[...].astype(F32))
    back = norm_back(grad, normed, factor, gain[0:1, :].astype(F32))
    keep[...] = back
    d_ref[...] = keep[pl.ds(pl.multiple_of(far * 32, 32), 32), :]
    low = back.astype(BF)
    low_ref[...] = low
    sums_ref[...] = sums_in[...]
    sums_ref[3:4, :] = jnp.sum(low.astype(F32), axis=0, keepdims=True)
    sums_ref[4:5, :] = jnp.sum(grad * normed, axis=0, keepdims=True)
    sums_ref[5:6, :] = jnp.sum(grad, axis=0, keepdims=True)


def parts(row):
    high = row.astype(BF)
    rest = row - high.astype(F32)
    middle = rest.astype(BF)
    return (high, middle, (rest - middle.astype(F32)).astype(BF))


def out_back_kernel(
    place, low, o, lse, wo_own, wo_oth, own_ref, oth_ref, d_ref, delta_ref, pack_ref, nat_ref
):
    shard = place[0]
    nat_ref[0:32, :] = low[0, 0:32, :]
    nat_ref[32:64, :] = low[1, 0:32, :]
    nat_ref[64:96, :] = low[0, 32:64, :]
    nat_ref[96:128, :] = low[1, 32:64, :]
    own, oth = nat_ref[:, half_at(shard, True)], nat_ref[:, half_at(shard, False)]
    own_ref[...] = own
    oth_ref[...] = oth
    d_out = (mm(own, wo_own[...], NT) + mm(oth, wo_oth[...], NT)).astype(BF)
    d_ref[...] = d_out
    turned = (d_out.astype(F32) * o[...]).T
    delta = jnp.concatenate(
        [
            jnp.sum(turned[head * HD : (head + 1) * HD], axis=0, keepdims=True)
            for head in range(HEADS)
        ],
        axis=1,
    )
    delta_ref[...] = delta
    rows = [d_out]
    for row in parts(lse[...]) + parts(delta):
        rows += [row[:, 0:COLS], row[:, COLS : 2 * COLS]]
    rows.append(jnp.zeros((4, COLS), BF))
    packed = jnp.concatenate(rows, axis=0)
    for index in range(RING):
        pack_ref[index] = packed


def query_grad_kernel(place, q, k, v, d_out, lse, delta, id_q, id_k, dq_ref, acc_ref):
    q_heads = by_head(q[place[1]].reshape(BLK, COLS) * BF(HD ** -0.5))
    d_heads = by_head(d_out[...])
    acc_ref[...] = jnp.zeros_like(acc_ref)

    @pl.loop(0, RING // 2)
    def _(step):
        blocks = pl.ds(step * 2, 2)
        keys, values = k[blocks].reshape(256, COLS), v[blocks].reshape(256, COLS)
        allowed = id_k[blocks].reshape(256, 1) == id_q[...]
        probs = jnp.where(allowed, jnp.exp(mm(keys, q_heads, NT) - lse[...]), 0.0)
        d_scores = (probs * (mm(values, d_heads, NT) - delta[...])).astype(BF)
        acc_ref[...] += mm(d_scores, keys, TN)

    lane = lax.broadcasted_iota(jnp.int32, (BLK, COLS), 1) // HD
    total = jnp.zeros((BLK, COLS), F32)
    for head in range(HEADS):
        total = jnp.where(lane == head, acc_ref[head * BLK : (head + 1) * BLK, :], total)
    dq_ref[...] = (total * HD ** -0.5).astype(BF)


def key_grad_kernel(
    place, q, k, v, dq, recv, ids, id_k, w_own, w_oth, d_ref, mine_ref, theirs_ref, part_ref
):
    shard, block = place[0], place[1]
    keys, values = k[block].reshape(BLK, COLS), v[block].reshape(BLK, COLS)
    own_ids = id_k[block]

    def step(index, carry):
        d_key, d_value = carry
        q_heads = by_head(q[index].reshape(BLK, COLS) * BF(HD ** -0.5))
        d_heads = by_head(recv[index, 0:BLK, :])
        tail = recv[index, BLK : BLK + 16, :].astype(F32)
        rows = [
            jnp.concatenate(
                [tail[at + side : at + side + 1] + tail[at + 2 + side : at + 3 + side]
                 + tail[at + 4 + side : at + 5 + side] for side in range(2)],
                axis=1,
            )
            for at in (0, 6)
        ]
        allowed = own_ids == ids[index]
        probs = jnp.where(allowed, jnp.exp(mm(keys, q_heads, NT) - rows[0]), 0.0)
        d_scores = (probs * (mm(values, d_heads, NT) - rows[1])).astype(BF)
        return d_key + mm(d_scores, q_heads), d_value + mm(probs.astype(BF), d_heads)

    start = jnp.zeros((BLK, COLS), F32)
    d_key, d_value = lax.fori_loop(0, RING, step, (start, start), unroll=2)
    d_ref[:, 0:COLS] = dq[...]
    d_ref[:, COLS : 2 * COLS] = d_key.astype(BF)
    d_ref[:, 2 * COLS : 3 * COLS] = d_value.astype(BF)
    for own, weight in ((True, w_own), (False, w_oth)):
        part_ref[:, half_at(shard, own)] = (
            mm(d_ref[:, 0:COLS], weight[0], NT)
            + mm(d_ref[:, COLS : 2 * COLS], weight[1], NT)
            + mm(d_ref[:, 2 * COLS : 3 * COLS], weight[2], NT)
        )
    split_rows(place, part_ref, mine_ref, theirs_ref)


def ring_sum(recv, rows):
    total = recv[0, rows, :].astype(F32)
    for index in range(1, RING):
        total = total + recv[index, rows, :].astype(F32)
    return total


def in_grads_kernel(
    place, tokens, d, d_pair, pair_in, ob, low, low_pair, sums, out_ref
):
    shard = place[0]
    rows = jnp.concatenate([tokens[:, half_at(shard, True)], pair_in[:, 256:768]], axis=0)
    grads = jnp.concatenate([d[...], d_pair[...]], axis=0)
    for part in range(3):
        term = mm(rows, grads[:, part * COLS : (part + 1) * COLS], TN).astype(BF)
        out_ref[:, part * 32 : part * 32 + 32, :] = term.reshape(RING, 32, COLS)
    heads = jnp.concatenate([ob[...], pair_in[:, 0:256]], axis=0)
    outs = jnp.concatenate([low[...], low_pair[...]], axis=0)
    for side in range(2):
        term = mm(heads, outs[:, side * COLS : (side + 1) * COLS], TN).astype(BF)
        out_ref[:, 96 + side * 16 : 112 + side * 16, :] = term.reshape(RING, 16, COLS)
    wide = grads.astype(F32)
    small = jnp.concatenate(
        [
            sums[0:6, :],
            jnp.sum(wide[:, 0:COLS], axis=0, keepdims=True),
            jnp.sum(wide[:, 2 * COLS : 3 * COLS], axis=0, keepdims=True),
            jnp.zeros((8, COLS), F32),
        ],
        axis=0,
    ).astype(BF)
    for index in range(RING):
        out_ref[index, 128:144, :] = small


def unit_total_kernel(place, recv, low_ref, bias_ref):
    low_ref[...] = ring_sum(recv, slice(0, 256)).astype(BF)
    bias_ref[...] = ring_sum(recv, slice(256, 272))


def total_kernel(place, recv, small_ref, out_ref):
    total = ring_sum(recv, slice(0, 144))
    small_ref[...] = total[128:144]
    low = total[0:128].astype(BF)
    for index in range(RING):
        out_ref[index] = low


def unpack_units_kernel(place, recv, up_ref, down_ref):
    for part in range(4):
        up_ref[:, part * COLS : (part + 1) * COLS] = (
            recv[:, part * 32 : part * 32 + 32, :].reshape(HALF, COLS).astype(F32)
        )
    for side in range(2):
        down_ref[:, side * COLS : (side + 1) * COLS] = (
            recv[:, 128 + side * 64 : 192 + side * 64, :].reshape(UNITS, COLS).astype(F32)
        )


def unpack_kernel(place, recv, in_ref, out_ref):
    for part in range(3):
        in_ref[part] = recv[:, part * 32 : part * 32 + 32, :].reshape(HALF, COLS).astype(F32)
    for side in range(2):
        out_ref[:, side * COLS : (side + 1) * COLS] = (
            recv[:, 96 + side * 16 : 112 + side * 16, :].reshape(COLS, COLS).astype(F32)
        )


def swap(value, axis, bit):
    size = lax.axis_size(axis)
    return lax.ppermute(value, axis, [(index, index ^ bit) for index in range(size)])


def pair_gather(value):
    return lax.all_gather(value, "tensor", axis=0, axis_index_groups=[[0, 1], [2, 3]])


def tensor_sum(mine, theirs):
    chip = (mine.astype(F32) + swap(theirs, "tensor", 1).astype(F32)).astype(BF)
    return chip, swap(chip, "tensor", 2)


def shards(
    tokens, segment_ids, w_qkv, b_qv, w_out, w_up, b_up, w_down, out_bias, ln_gain, ln_bias, cotangent
):
    shard, block, tensor = (lax.axis_index(name) for name in ("shard", "context", "tensor"))
    core, far = tensor % 2, tensor // 2
    place = jnp.stack([shard, block, core, far]).astype(jnp.int32)
    w_in = jnp.transpose(w_qkv[0], (1, 0, 2))
    w_out, w_up, w_down = w_out[0], w_up[0], w_down[0]
    extra, gain, shift = out_bias[0], ln_gain[0], ln_bias[0]
    together = lax.optimization_barrier

    up_rows = lax.dynamic_slice_in_dim(w_up, block * 32, 32, 0)
    down_rows = lax.dynamic_slice_in_dim(w_down, block * 64, 64, 0)
    unit_rows = swap(
        jnp.concatenate([up_rows[:, :HALF], up_rows[:, HALF:], down_rows], axis=0), "shard", 1
    )
    other = lax.all_gather(unit_rows, "context", axis=0)
    in_oth = swap(w_in, "shard", 1)
    out_oth = swap(w_out, "shard", 1)

    spread = jnp.broadcast_to(
        lax.dynamic_slice_in_dim(tokens, core * 64, 64, 0)[None], (RING, 64, D)
    )
    spread, _ = together((spread, unit_rows))
    x_mine = lax.all_to_all(spread, "context", 0, 0, tiled=True)
    x_mine, in_oth, out_oth = together((x_mine, in_oth, out_oth))
    x_sib = swap(x_mine, "tensor", 1)

    id_q = lax.dynamic_slice_in_dim(segment_ids, block * BLK, BLK, 0)
    id_column = segment_ids.reshape(RING, BLK, 1)
    id_heads = jnp.tile(segment_ids.reshape(RING, 1, BLK), (1, 1, HEADS))
    all_heads = ((RING, 2, 64, COLS), BF)
    halves = [((64, D), BF), ((64, D), BF)]
    whole = pltpu.VMEM((BLK, D), F32)
    q, k, v, o, ob, lse, mine, theirs = call(
        attend_kernel, 10,
        [all_heads] * 3 + [((BLK, COLS), F32), ((BLK, COLS), BF), ((1, HEADS * BLK), F32)] + halves,
        place, x_mine, x_sib, w_in, in_oth, b_qv[0], id_q[:, None], segment_ids[None, :],
        w_out, out_oth,
        scratch=[whole], vmem=60,
    )
    chip, recv = tensor_sum(mine, theirs)
    first, low_mid = call(
        first_norm_kernel, 1, [((64, D), F32), ((64, D), BF)],
        place, tokens, chip, recv, extra, gain, shift,
    )
    hb = pair_gather(low_mid).reshape(BLK, D)
    ub, slope, mine, theirs = call(
        up_down_kernel, 2, [((BLK, UNITS), BF), ((BLK, UNITS), F32)] + halves,
        place, hb, w_up, w_down, other, b_up,
        scratch=[whole],
    )
    away = (1 - shard) * HALF
    pair_in = swap(
        jnp.concatenate([ob, lax.dynamic_slice_in_dim(tokens, away, HALF, 1)], axis=1), "shard", 1
    )
    pair_fwd = swap(
        jnp.concatenate([lax.dynamic_slice_in_dim(hb, away, HALF, 1), ub], axis=1), "shard", 1
    )
    chip, recv = tensor_sum(mine, theirs)
    hidden_out, dx, low_second, sums = call(
        second_norm_kernel, 2,
        [((32, D), F32), ((64, D), F32), ((64, D), BF), ((8, D), F32)],
        place, first, chip, recv, extra, gain, shift, cotangent,
        scratch=[pltpu.VMEM((64, D), F32)],
    )
    dz = pair_gather(low_second).reshape(BLK, D)
    pair_dz = swap(lax.dynamic_slice_in_dim(dz, away, HALF, 1), "shard", 1)
    da, mine, theirs = call(
        down_up_kernel, 2, [((BLK, UNITS), BF)] + halves,
        place, dz, slope, w_up, w_down, other,
        scratch=[whole],
    )
    pair_da = swap(da, "shard", 1)
    chip, recv = tensor_sum(mine, theirs)
    pair_da, chip = together((pair_da, chip))
    (unit_grads,) = call(
        unit_grads_kernel, 3, [((RING, 272, COLS), BF)],
        place, hb, da, ub, dz, pair_fwd, pair_dz, pair_da,
    )
    recv, unit_grads = together((recv, unit_grads))
    unit_recv = lax.all_to_all(unit_grads, "context", 0, 0, tiled=True)
    d_first, low_first, sums = call(
        first_back_kernel, 1.5,
        [((32, D), F32), ((64, D), BF), ((8, D), F32)],
        place, first, dx, chip, recv, gain, shift, sums,
        scratch=[pltpu.VMEM((64, D), F32)], vmem=60,
    )
    low_pairs = pair_gather(low_first)
    low_own, low_oth, d_out, delta, packed = call(
        out_back_kernel, 1.5,
        [
            ((BLK, HALF), BF), ((BLK, HALF), BF), ((BLK, COLS), BF), ((1, HEADS * BLK), F32),
            ((RING, 144, COLS), BF),
        ],
        place, low_pairs, o, lse, w_out, out_oth,
        scratch=[pltpu.VMEM((BLK, D), BF)],
    )
    packed, unit_recv = together((packed, unit_recv))
    packs = lax.all_to_all(packed, "context", 0, 0, tiled=True)
    unit_total, unit_small = call(
        unit_total_kernel, 1, [((COLS, COLS), BF), ((16, COLS), F32)], place, unit_recv
    )
    unit_all = lax.all_gather(unit_total, "context", axis=0)
    packs, unit_total = together((packs, unit_total))
    low_pair = swap(low_oth, "shard", 1)
    sums = sums + swap(sums, "tensor", 1)
    sums = lax.dynamic_slice_in_dim(sums, tensor * COLS, COLS, 1)
    sums = sums + swap(sums, "shard", 1)
    (dq,) = call(
        query_grad_kernel, 5, [((BLK, COLS), BF)],
        place, q, k, v, d_out, lse, delta, jnp.tile(id_q[None, :], (1, HEADS)), id_column,
        scratch=[pltpu.VMEM((HEADS * BLK, COLS), F32)], vmem=60,
    )
    d_mixed, mine, theirs = call(
        key_grad_kernel, 6, [((BLK, 3 * COLS), BF)] + halves,
        place, q, k, v, dq, packs, id_heads, id_column, w_in, in_oth,
        scratch=[whole], vmem=60,
    )
    d_pair = swap(d_mixed, "shard", 1)
    chip = mine.astype(F32) + swap(theirs, "tensor", 1).astype(F32)
    chip_far = lax.dynamic_slice_in_dim(chip, (1 - far) * 32, 32, 0).astype(BF)
    chip_near = lax.dynamic_slice_in_dim(chip, far * 32, 32, 0)
    grad_tokens = d_first + (chip_near + swap(chip_far, "tensor", 2).astype(F32))
    (in_grads,) = call(
        in_grads_kernel, 2.5, [((RING, 144, COLS), BF)],
        place, tokens, d_mixed, d_pair, pair_in, ob, low_own, low_pair, sums,
    )
    recv = lax.all_to_all(in_grads, "context", 0, 0, tiled=True)
    small, totals = call(
        total_kernel, 2, [((16, COLS), F32), ((RING, 128, COLS), BF)], place, recv
    )
    recv = lax.all_to_all(totals, "context", 0, 0, tiled=True)
    grad_in, grad_w_out = call(
        unpack_kernel, 2, [((3, HALF, COLS), F32), ((COLS, HALF), F32)], place, recv
    )
    grad_w_up, grad_w_down = call(
        unpack_units_kernel, 2, [((HALF, UNITS), F32), ((UNITS, HALF), F32)], place, unit_all
    )
    return (
        hidden_out,
        grad_tokens,
        jnp.transpose(grad_in, (1, 0, 2))[None],
        grad_w_out[None],
        grad_w_up[None],
        grad_w_down[None],
        small[6:8][None],
        unit_small[0:4].reshape(1, UNITS),
        jnp.stack([small[3], small[0]])[None],
        jnp.stack([small[4], small[1]])[None],
        jnp.stack([small[5], small[2]])[None],
    )


def solution(mesh):
    rows = P(("shard", "context"), None)
    own_rows = P(("shard", "context", "tensor"), None)
    by_column = P(None, None, "tensor")
    in_specs = (
        rows,
        P("shard"),
        P(None, "shard", None, "tensor"),
        by_column,
        P(None, "tensor", "shard"),
        P(None, "shard", "tensor"),
        P(None, "tensor"),
        P(None, "tensor", "shard"),
        P(),
        P(),
        P(),
        rows,
    )
    out_specs = (
        own_rows,
        own_rows,
        P(None, "shard", None, "tensor"),
        P(None, "tensor", "shard"),
        P(None, "shard", "tensor"),
        P(None, "tensor", "shard"),
        by_column,
        P(None, "tensor"),
        by_column,
        by_column,
        by_column,
    )
    return jax.shard_map(shards, mesh=mesh, in_specs=in_specs, out_specs=out_specs, check_vma=False)
```

```python
import functools

import jax
import jax.numpy as jnp
from jax import lax
from jax.experimental import pallas as pl
from jax.experimental.pallas import tpu as pltpu
from jax.sharding import PartitionSpec as P

HD = 64
HEADS = 4
BLK = 128
LEN = 2048
D = 1024
HALF = 512
COLS = 256
UNITS = 1024
RING = 16
EPSILON = 1e-05
NEGATIVE = -1e30
ROOT_HALF = 0.7071067811865476
DENSITY = 0.3989422804014327
BF = jnp.bfloat16
F32 = jnp.float32

NN = (((1,), (0,)), ((), ()))
NT = (((1,), (1,)), ((), ()))
TN = (((0,), (0,)), ((), ()))


def mm(a, b, dims=NN):
    return lax.dot_general(a, b, dims, preferred_element_type=F32)


def call(kernel, micros, outs, scalars, *args, scratch=(), vmem=20):
    specs = [pl.BlockSpec(memory_space=pltpu.SMEM)]
    specs += [pl.BlockSpec(memory_space=pltpu.VMEM)] * len(args)
    return pl.pallas_call(
        kernel,
        out_shape=[jax.ShapeDtypeStruct(shape, dtype) for shape, dtype in outs],
        in_specs=specs,
        out_specs=[pl.BlockSpec(memory_space=pltpu.VMEM)] * len(outs),
        scratch_shapes=list(scratch),
        compiler_params=pltpu.CompilerParams(vmem_limit_bytes=vmem << 20),
        cost_estimate=pl.CostEstimate(
            flops=int(micros * 1.1e9), bytes_accessed=int(micros * 3e6), transcendentals=0
        ),
    )(scalars, *args)


def half_at(shard, own):
    return pl.ds(pl.multiple_of((shard if own else 1 - shard) * HALF, HALF), HALF)


def by_head(rows):
    lane = lax.broadcasted_iota(jnp.int32, rows.shape, 1) // HD
    return jnp.concatenate(
        [jnp.where(lane == head, rows, jnp.zeros_like(rows)) for head in range(HEADS)], axis=0
    )


def norm_rows(summed, gain, shift):
    centred = summed - jnp.mean(summed, axis=-1, keepdims=True)
    factor = lax.rsqrt(jnp.mean(centred * centred, axis=-1, keepdims=True) + EPSILON)
    normed = centred * factor
    return normed * gain + shift, normed, factor


def norm_back(incoming, normed, factor, gain):
    scaled = incoming * gain
    centre = jnp.mean(scaled, axis=-1, keepdims=True)
    along = jnp.mean(scaled * normed, axis=-1, keepdims=True)
    return factor * (scaled - centre - normed * along)


def split_rows(place, rows_ref, mine_ref, theirs_ref):
    core = place[2]
    for part in range(2):
        mine = pl.multiple_of(part * 64 + core * 32, 32)
        theirs = pl.multiple_of(part * 64 + (1 - core) * 32, 32)
        mine_ref[pl.ds(part * 32, 32), :] = rows_ref[pl.ds(mine, 32), :].astype(BF)
        theirs_ref[pl.ds(part * 32, 32), :] = rows_ref[pl.ds(theirs, 32), :].astype(BF)


def split_halves(place, rows_ref, mine_ref, theirs_ref):
    core = place[2]
    mine_ref[...] = rows_ref[pl.ds(pl.multiple_of(core * 64, 64), 64), :].astype(BF)
    theirs_ref[...] = rows_ref[pl.ds(pl.multiple_of((1 - core) * 64, 64), 64), :].astype(BF)


def core_rows(place, ref):
    core = place[2]
    return jnp.concatenate(
        [ref[pl.ds(pl.multiple_of(part * 64 + core * 32, 32), 32), :] for part in range(2)], axis=0
    )


def attend_kernel(
    place, x_mine, x_sib, w_own, w_oth, b_qv, id_q, id_k, wo_own, wo_oth,
    q_ref, k_ref, v_ref, o_ref, ob_ref, lse_ref, mine_ref, theirs_ref, part_ref,
):
    shard, block, core = place[0], place[1], place[2]
    biases = b_qv[...].astype(F32)
    own, oth = half_at(shard, True), half_at(shard, False)

    @pl.loop(0, RING // 4)
    def _(step):
        blocks = pl.ds(step * 4, 4)
        for x, side in ((x_mine, core), (x_sib, 1 - core)):
            x_own = x[blocks, :, own].reshape(256, HALF)
            x_oth = x[blocks, :, oth].reshape(256, HALF)
            queries = mm(x_own, w_own[0]) + mm(x_oth, w_oth[0]) + biases[0:1]
            keys = mm(x_own, w_own[1]) + mm(x_oth, w_oth[1])
            values = mm(x_own, w_own[2]) + mm(x_oth, w_oth[2]) + biases[1:2]
            q_ref[blocks, side] = queries.astype(BF).reshape(4, 64, COLS)
            k_ref[blocks, side] = keys.astype(BF).reshape(4, 64, COLS)
            v_ref[blocks, side] = values.astype(BF).reshape(4, 64, COLS)

    keys, values = k_ref[...].reshape(LEN, COLS), v_ref[...].reshape(LEN, COLS)
    q_heads = by_head(q_ref[block].reshape(BLK, COLS) * BF(HD ** -0.5))
    allowed = id_k[place[1]] == jnp.concatenate(
        [id_q[index][:, 0:BLK] for index in range(RING)], axis=1
    )
    lane = lax.broadcasted_iota(jnp.int32, (BLK, COLS), 1) // HD
    out = jnp.zeros((BLK, COLS), F32)
    for head in range(HEADS):
        scores = mm(q_heads[head * BLK : (head + 1) * BLK], keys, NT)
        scores = jnp.where(allowed, scores, NEGATIVE)
        highest = jnp.max(scores, axis=-1, keepdims=True)
        weights = jnp.exp(scores - highest)
        total = jnp.sum(weights, axis=-1, keepdims=True)
        mixed = mm(weights.astype(BF), values) / total
        out = jnp.where(lane == head, mixed, out)
        column = jnp.broadcast_to(highest + jnp.log(total), (BLK, BLK))
        lse_ref[:, head * BLK : (head + 1) * BLK] = column.T[0:1, :]
    o_ref[...] = out
    low = out.astype(BF)
    ob_ref[...] = low
    part_ref[:, own] = mm(low, wo_own[...])
    part_ref[:, oth] = mm(low, wo_oth[...])
    split_rows(place, part_ref, mine_ref, theirs_ref)


def first_norm(summed, gain, shift):
    return norm_rows(summed[...], gain[0:1, :].astype(F32), shift[0:1, :].astype(F32))


def first_norm_kernel(place, tokens, chip, recv, extra, gain, shift, s_ref, hb_ref):
    branch = chip[...].astype(F32) + recv[...].astype(F32) + extra[0:1, :].astype(F32)
    s_ref[...] = core_rows(place, tokens).astype(F32) + branch
    hb_ref[...] = first_norm(s_ref, gain, shift)[0].astype(BF)


def other_up(other, side):
    return other[:, side * 32 : side * 32 + 32, :].reshape(HALF, HALF)


def other_down(other):
    return other[:, 64:128, :].reshape(UNITS, HALF)


def up_down_kernel(
    place, hb, up_own, down_own, other, b_up,
    ub_ref, slope_ref, mine_ref, theirs_ref, part_ref,
):
    shard = place[0]
    own, oth = hb[:, half_at(shard, True)], hb[:, half_at(shard, False)]
    for side in range(2):
        cols = pl.ds(side * HALF, HALF)
        before = mm(own, up_own[:, cols]) + mm(oth, other_up(other, side)) + b_up[:, cols].astype(F32)
        bell = 0.5 * (1.0 + lax.erf(before * ROOT_HALF))
        ub_ref[:, cols] = (before * bell).astype(BF)
        slope_ref[:, cols] = bell + before * DENSITY * jnp.exp(-0.5 * before * before)
    after = ub_ref[...]
    part_ref[:, half_at(shard, True)] = mm(after, down_own[...])
    part_ref[:, half_at(shard, False)] = mm(after, other_down(other))
    split_halves(place, part_ref, mine_ref, theirs_ref)


def second_norm_kernel(
    place, first, chip, recv, extra, gain, shift, cot, out_ref, dx_ref, dz_ref, sums_ref, keep
):
    far = place[3]
    middle = first_norm(first, gain, shift)[0]
    gains = gain[1:2, :].astype(F32)
    branch = chip[...].astype(F32) + recv[...].astype(F32) + extra[1:2, :].astype(F32)
    hidden, normed, factor = norm_rows(middle + branch, gains, shift[1:2, :].astype(F32))
    keep[...] = hidden
    out_ref[...] = keep[pl.ds(pl.multiple_of(far * 32, 32), 32), :]
    grad = core_rows(place, cot)
    back = norm_back(grad, normed, factor, gains)
    dx_ref[...] = back
    low = back.astype(BF)
    dz_ref[...] = low
    sums_ref[0:1, :] = jnp.sum(low.astype(F32), axis=0, keepdims=True)
    sums_ref[1:2, :] = jnp.sum(grad * normed, axis=0, keepdims=True)
    sums_ref[2:3, :] = jnp.sum(grad, axis=0, keepdims=True)
    sums_ref[3:8, :] = jnp.zeros((5, D), F32)


def down_up_kernel(
    place, dz, slope, up_own, down_own, other, da_ref, mine_ref, theirs_ref, part_ref
):
    shard = place[0]
    own, oth = dz[:, half_at(shard, True)], dz[:, half_at(shard, False)]
    after = mm(own, down_own[...], NT) + mm(oth, other_down(other), NT)
    da_ref[...] = (after * slope[...]).astype(BF)
    before = da_ref[...]
    part_ref[:, half_at(shard, True)] = mm(before, up_own[...], NT)
    part_ref[:, half_at(shard, False)] = sum(
        mm(before[:, side * HALF : (side + 1) * HALF], other_up(other, side), NT) for side in range(2)
    )
    split_halves(place, part_ref, mine_ref, theirs_ref)


def unit_grads_kernel(place, hb, da, ub, dz, pair_fwd, pair_dz, pair_da, out_ref, bias_ref):
    shard = place[0]
    rows = jnp.concatenate([hb[:, half_at(shard, True)], pair_fwd[:, 0:512]], axis=0)
    units = jnp.concatenate([da[...], pair_da[...]], axis=0)
    after = jnp.concatenate([ub[...], pair_fwd[:, 512:1536]], axis=0)
    grads = jnp.concatenate([dz[:, half_at(shard, True)], pair_dz[...]], axis=0)
    for part in range(4):
        cols = slice(part * COLS, (part + 1) * COLS)
        term = mm(rows, units[:, cols], TN).astype(BF)
        out_ref[:, part * 32 : part * 32 + 32, :] = term.reshape(RING, 32, COLS)
    for side in range(2):
        cols = slice(side * COLS, (side + 1) * COLS)
        term = mm(after, grads[:, cols], TN).astype(BF)
        out_ref[:, 128 + side * 64 : 192 + side * 64, :] = term.reshape(RING, 64, COLS)
    total = jnp.sum(units.astype(F32), axis=0, keepdims=True)
    bias_ref[...] = jnp.concatenate(
        [total[:, part * COLS : (part + 1) * COLS] for part in range(4)]
        + [jnp.zeros((4, COLS), F32)],
        axis=0,
    )


def first_back_kernel(
    place, first, dx, chip, recv, gain, shift, sums_in, d_ref, low_ref, sums_ref, keep
):
    far = place[3]
    _, normed, factor = first_norm(first, gain, shift)
    grad = dx[...] + (chip[...].astype(F32) + recv[...].astype(F32))
    back = norm_back(grad, normed, factor, gain[0:1, :].astype(F32))
    keep[...] = back
    d_ref[...] = keep[pl.ds(pl.multiple_of(far * 32, 32), 32), :]
    low = back.astype(BF)
    low_ref[...] = low
    sums_ref[...] = sums_in[...]
    sums_ref[3:4, :] = jnp.sum(low.astype(F32), axis=0, keepdims=True)
    sums_ref[4:5, :] = jnp.sum(grad * normed, axis=0, keepdims=True)
    sums_ref[5:6, :] = jnp.sum(grad, axis=0, keepdims=True)


def parts(row):
    high = row.astype(BF)
    rest = row - high.astype(F32)
    middle = rest.astype(BF)
    return (high, middle, (rest - middle.astype(F32)).astype(BF))


def out_back_kernel(
    place, low, o, lse, wo_own, wo_oth, own_ref, oth_ref, d_ref, delta_ref, pack_ref, nat_ref
):
    shard = place[0]
    nat_ref[0:32, :] = low[0, 0:32, :]
    nat_ref[32:64, :] = low[1, 0:32, :]
    nat_ref[64:96, :] = low[0, 32:64, :]
    nat_ref[96:128, :] = low[1, 32:64, :]
    own, oth = nat_ref[:, half_at(shard, True)], nat_ref[:, half_at(shard, False)]
    own_ref[...] = own
    oth_ref[...] = oth
    d_out = (mm(own, wo_own[...], NT) + mm(oth, wo_oth[...], NT)).astype(BF)
    d_ref[...] = d_out
    turned = (d_out.astype(F32) * o[...]).T
    delta = jnp.concatenate(
        [
            jnp.sum(turned[head * HD : (head + 1) * HD], axis=0, keepdims=True)
            for head in range(HEADS)
        ],
        axis=1,
    )
    delta_ref[...] = delta
    rows = [d_out]
    for row in parts(lse[...]) + parts(delta):
        rows += [row[:, 0:COLS], row[:, COLS : 2 * COLS]]
    rows.append(jnp.zeros((4, COLS), BF))
    packed = jnp.concatenate(rows, axis=0)
    for index in range(RING):
        pack_ref[index] = packed


def query_grad_kernel(place, q, k, v, d_out, lse, delta, id_q, id_k, dq_ref, acc_ref):
    q_heads = by_head(q[place[1]].reshape(BLK, COLS) * BF(HD ** -0.5))
    d_heads = by_head(d_out[...])
    acc_ref[...] = jnp.zeros_like(acc_ref)

    @pl.loop(0, RING // 2)
    def _(step):
        blocks = pl.ds(step * 2, 2)
        keys, values = k[blocks].reshape(256, COLS), v[blocks].reshape(256, COLS)
        allowed = id_k[blocks].reshape(256, 1) == id_q[place[1]]
        probs = jnp.where(allowed, jnp.exp(mm(keys, q_heads, NT) - lse[...]), 0.0)
        d_scores = (probs * (mm(values, d_heads, NT) - delta[...])).astype(BF)
        acc_ref[...] += mm(d_scores, keys, TN)

    lane = lax.broadcasted_iota(jnp.int32, (BLK, COLS), 1) // HD
    total = jnp.zeros((BLK, COLS), F32)
    for head in range(HEADS):
        total = jnp.where(lane == head, acc_ref[head * BLK : (head + 1) * BLK, :], total)
    dq_ref[...] = (total * HD ** -0.5).astype(BF)


def key_grad_kernel(
    place, q, k, v, dq, recv, ids, id_k, w_own, w_oth, d_ref, mine_ref, theirs_ref, part_ref
):
    shard, block = place[0], place[1]
    keys, values = k[block].reshape(BLK, COLS), v[block].reshape(BLK, COLS)
    own_ids = id_k[block]

    def step(index, carry):
        d_key, d_value = carry
        q_heads = by_head(q[index].reshape(BLK, COLS) * BF(HD ** -0.5))
        d_heads = by_head(recv[index, 0:BLK, :])
        tail = recv[index, BLK : BLK + 16, :].astype(F32)
        rows = [
            jnp.concatenate(
                [tail[at + side : at + side + 1] + tail[at + 2 + side : at + 3 + side]
                 + tail[at + 4 + side : at + 5 + side] for side in range(2)],
                axis=1,
            )
            for at in (0, 6)
        ]
        allowed = own_ids == ids[index]
        probs = jnp.where(allowed, jnp.exp(mm(keys, q_heads, NT) - rows[0]), 0.0)
        d_scores = (probs * (mm(values, d_heads, NT) - rows[1])).astype(BF)
        return d_key + mm(d_scores, q_heads), d_value + mm(probs.astype(BF), d_heads)

    start = jnp.zeros((BLK, COLS), F32)
    d_key, d_value = lax.fori_loop(0, RING, step, (start, start), unroll=2)
    d_ref[:, 0:COLS] = dq[...]
    d_ref[:, COLS : 2 * COLS] = d_key.astype(BF)
    d_ref[:, 2 * COLS : 3 * COLS] = d_value.astype(BF)
    for own, weight in ((True, w_own), (False, w_oth)):
        part_ref[:, half_at(shard, own)] = (
            mm(d_ref[:, 0:COLS], weight[0], NT)
            + mm(d_ref[:, COLS : 2 * COLS], weight[1], NT)
            + mm(d_ref[:, 2 * COLS : 3 * COLS], weight[2], NT)
        )
    split_rows(place, part_ref, mine_ref, theirs_ref)


def ring_sum(recv, rows):
    total = recv[0, rows, :].astype(F32)
    for index in range(1, RING):
        total = total + recv[index, rows, :].astype(F32)
    return total


def in_grads_kernel(
    place, tokens, d, d_pair, pair_in, ob, low, low_pair, sums, unit_sums, out_ref
):
    shard = place[0]
    rows = jnp.concatenate([tokens[:, half_at(shard, True)], pair_in[:, 256:768]], axis=0)
    grads = jnp.concatenate([d[...], d_pair[...]], axis=0)
    for part in range(3):
        term = mm(rows, grads[:, part * COLS : (part + 1) * COLS], TN).astype(BF)
        out_ref[:, part * 32 : part * 32 + 32, :] = term.reshape(RING, 32, COLS)
    heads = jnp.concatenate([ob[...], pair_in[:, 0:256]], axis=0)
    outs = jnp.concatenate([low[...], low_pair[...]], axis=0)
    for side in range(2):
        term = mm(heads, outs[:, side * COLS : (side + 1) * COLS], TN).astype(BF)
        out_ref[:, 96 + side * 16 : 112 + side * 16, :] = term.reshape(RING, 16, COLS)
    wide = grads.astype(F32)
    small = jnp.concatenate(
        [
            sums[0:6, :],
            jnp.sum(wide[:, 0:COLS], axis=0, keepdims=True),
            jnp.sum(wide[:, 2 * COLS : 3 * COLS], axis=0, keepdims=True),
            unit_sums[...],
        ],
        axis=0,
    ).astype(BF)
    for index in range(RING):
        out_ref[index, 128:144, :] = small


def unit_total_kernel(place, recv, low_ref):
    low_ref[...] = ring_sum(recv, slice(0, 256)).astype(BF)


def total_kernel(place, recv, small_ref, out_ref):
    total = ring_sum(recv, slice(0, 144))
    small_ref[...] = total[128:144]
    low = total[0:128].astype(BF)
    for index in range(RING):
        out_ref[index] = low


def unpack_units_kernel(place, recv, up_ref, down_ref):
    for part in range(4):
        up_ref[:, part * COLS : (part + 1) * COLS] = (
            recv[:, part * 32 : part * 32 + 32, :].reshape(HALF, COLS).astype(F32)
        )
    for side in range(2):
        down_ref[:, side * COLS : (side + 1) * COLS] = (
            recv[:, 128 + side * 64 : 192 + side * 64, :].reshape(UNITS, COLS).astype(F32)
        )


def unpack_kernel(place, recv, in_ref, out_ref):
    for part in range(3):
        in_ref[part] = recv[:, part * 32 : part * 32 + 32, :].reshape(HALF, COLS).astype(F32)
    for side in range(2):
        out_ref[:, side * COLS : (side + 1) * COLS] = (
            recv[:, 96 + side * 16 : 112 + side * 16, :].reshape(COLS, COLS).astype(F32)
        )


def swap(value, axis, bit):
    size = lax.axis_size(axis)
    return lax.ppermute(value, axis, [(index, index ^ bit) for index in range(size)])


def pair_gather(value):
    return lax.all_gather(value, "tensor", axis=0, axis_index_groups=[[0, 1], [2, 3]])


def tensor_sum(mine, theirs):
    chip = (mine.astype(F32) + swap(theirs, "tensor", 1).astype(F32)).astype(BF)
    return chip, swap(chip, "tensor", 2)


def shards(
    tokens, segment_ids, w_qkv, b_qv, w_out, w_up, b_up, w_down, out_bias, ln_gain, ln_bias, cotangent
):
    shard, block, tensor = (lax.axis_index(name) for name in ("shard", "context", "tensor"))
    core, far = tensor % 2, tensor // 2
    place = jnp.stack([shard, block, core, far]).astype(jnp.int32)
    w_in = jnp.transpose(w_qkv[0], (1, 0, 2))
    w_out, w_up, w_down = w_out[0], w_up[0], w_down[0]
    extra, gain, shift = out_bias[0], ln_gain[0], ln_bias[0]
    together = lax.optimization_barrier

    up_rows = lax.dynamic_slice_in_dim(w_up, block * 32, 32, 0)
    down_rows = lax.dynamic_slice_in_dim(w_down, block * 64, 64, 0)
    unit_rows = swap(
        jnp.concatenate([up_rows[:, :HALF], up_rows[:, HALF:], down_rows], axis=0), "shard", 1
    )
    other = lax.all_gather(unit_rows, "context", axis=0)
    w_in_late, _ = together((w_in, unit_rows))
    in_oth = swap(w_in_late, "shard", 1)
    out_oth = swap(w_out, "shard", 1)

    spread = jnp.broadcast_to(
        jnp.where(core == 0, tokens[0:64], tokens[64:128])[None], (RING, 64, D)
    )
    x_mine = lax.all_to_all(spread, "context", 0, 0, tiled=True)
    x_mine, in_oth, out_oth = together((x_mine, in_oth, out_oth))
    x_sib = swap(x_mine, "tensor", 1)

    id_column = segment_ids.reshape(RING, BLK, 1)
    id_heads = jnp.tile(segment_ids.reshape(RING, 1, BLK), (1, 1, HEADS))
    all_heads = ((RING, 2, 64, COLS), BF)
    halves = [((64, D), BF), ((64, D), BF)]
    whole = pltpu.VMEM((BLK, D), F32)
    q, k, v, o, ob, lse, mine, theirs = call(
        attend_kernel, 10,
        [all_heads] * 3 + [((BLK, COLS), F32), ((BLK, COLS), BF), ((1, HEADS * BLK), F32)] + halves,
        place, x_mine, x_sib, w_in, in_oth, b_qv[0], id_heads, id_column,
        w_out, out_oth,
        scratch=[whole], vmem=60,
    )
    chip, recv = tensor_sum(mine, theirs)
    first, low_mid = call(
        first_norm_kernel, 1, [((64, D), F32), ((64, D), BF)],
        place, tokens, chip, recv, extra, gain, shift,
    )
    hb = pair_gather(low_mid).reshape(BLK, D)
    ub, slope, mine, theirs = call(
        up_down_kernel, 2, [((BLK, UNITS), BF), ((BLK, UNITS), F32)] + halves,
        place, hb, w_up, w_down, other, b_up,
        scratch=[whole],
    )
    away = (1 - shard) * HALF
    pair_in = swap(
        jnp.concatenate([ob, lax.dynamic_slice_in_dim(tokens, away, HALF, 1)], axis=1), "shard", 1
    )
    pair_fwd = swap(
        jnp.concatenate([lax.dynamic_slice_in_dim(hb, away, HALF, 1), ub], axis=1), "shard", 1
    )
    chip, recv = tensor_sum(mine, theirs)
    hidden_out, dx, low_second, sums = call(
        second_norm_kernel, 2,
        [((32, D), F32), ((64, D), F32), ((64, D), BF), ((8, D), F32)],
        place, first, chip, recv, extra, gain, shift, cotangent,
        scratch=[pltpu.VMEM((64, D), F32)],
    )
    dz = pair_gather(low_second).reshape(BLK, D)
    pair_dz = swap(lax.dynamic_slice_in_dim(dz, away, HALF, 1), "shard", 1)
    da, mine, theirs = call(
        down_up_kernel, 2, [((BLK, UNITS), BF)] + halves,
        place, dz, slope, w_up, w_down, other,
        scratch=[whole],
    )
    pair_da = swap(da, "shard", 1)
    mine, pair_fwd = together((mine, pair_fwd))
    chip, recv = tensor_sum(mine, theirs)
    d_first, low_first, sums = call(
        first_back_kernel, 1.5,
        [((32, D), F32), ((64, D), BF), ((8, D), F32)],
        place, first, dx, chip, recv, gain, shift, sums,
        scratch=[pltpu.VMEM((64, D), F32)], vmem=60,
    )
    low_pairs = pair_gather(low_first)
    low_own, low_oth, d_out, delta, packed = call(
        out_back_kernel, 1.5,
        [
            ((BLK, HALF), BF), ((BLK, HALF), BF), ((BLK, COLS), BF), ((1, HEADS * BLK), F32),
            ((RING, 144, COLS), BF),
        ],
        place, low_pairs, o, lse, w_out, out_oth,
        scratch=[pltpu.VMEM((BLK, D), BF)],
    )
    packs = lax.all_to_all(packed, "context", 0, 0, tiled=True)
    (dq,) = call(
        query_grad_kernel, 5, [((BLK, COLS), BF)],
        place, q, k, v, d_out, lse, delta, id_heads, id_column,
        scratch=[pltpu.VMEM((HEADS * BLK, COLS), F32)], vmem=60,
    )
    hb, dq = together((hb, dq))
    unit_grads, unit_small = call(
        unit_grads_kernel, 3, [((RING, 256, COLS), BF), ((8, COLS), F32)],
        place, hb, da, ub, dz, pair_fwd, pair_dz, pair_da,
    )
    packs, unit_grads, dq = together((packs, unit_grads, dq))
    unit_recv = lax.all_to_all(unit_grads, "context", 0, 0, tiled=True)
    low_pair = swap(low_oth, "shard", 1)
    sums = sums + swap(sums, "tensor", 1)
    sums = lax.dynamic_slice_in_dim(sums, tensor * COLS, COLS, 1)
    sums = sums + swap(sums, "shard", 1)
    d_mixed, mine, theirs = call(
        key_grad_kernel, 6, [((BLK, 3 * COLS), BF)] + halves,
        place, q, k, v, dq, packs, id_heads, id_column, w_in, in_oth,
        scratch=[whole], vmem=60,
    )
    d_pair = swap(d_mixed, "shard", 1)
    chip = mine.astype(F32) + swap(theirs, "tensor", 1).astype(F32)
    chip_far = lax.dynamic_slice_in_dim(chip, (1 - far) * 32, 32, 0).astype(BF)
    chip_near = lax.dynamic_slice_in_dim(chip, far * 32, 32, 0)
    grad_tokens = d_first + (chip_near + swap(chip_far, "tensor", 2).astype(F32))
    (in_grads,) = call(
        in_grads_kernel, 2.5, [((RING, 144, COLS), BF)],
        place, tokens, d_mixed, d_pair, pair_in, ob, low_own, low_pair, sums, unit_small,
    )
    in_grads, unit_recv = together((in_grads, unit_recv))
    recv = lax.all_to_all(in_grads, "context", 0, 0, tiled=True)
    (unit_total,) = call(unit_total_kernel, 1, [((COLS, COLS), BF)], place, unit_recv)
    unit_all = lax.all_gather(unit_total, "context", axis=0)
    recv, _ = together((recv, unit_total))
    small, totals = call(
        total_kernel, 2, [((16, COLS), F32), ((RING, 128, COLS), BF)], place, recv
    )
    recv = lax.all_to_all(totals, "context", 0, 0, tiled=True)
    grad_in, grad_w_out = call(
        unpack_kernel, 2, [((3, HALF, COLS), F32), ((COLS, HALF), F32)], place, recv
    )
    grad_w_up, grad_w_down = call(
        unpack_units_kernel, 2, [((HALF, UNITS), F32), ((UNITS, HALF), F32)],
        place, unit_all, vmem=60,
    )
    return (
        hidden_out,
        grad_tokens,
        jnp.transpose(grad_in, (1, 0, 2))[None],
        grad_w_out[None],
        grad_w_up[None],
        grad_w_down[None],
        small[6:8][None],
        small[8:12].reshape(1, UNITS),
        jnp.stack([small[3], small[0]])[None],
        jnp.stack([small[4], small[1]])[None],
        jnp.stack([small[5], small[2]])[None],
    )


def solution(mesh):
    rows = P(("shard", "context"), None)
    own_rows = P(("shard", "context", "tensor"), None)
    by_column = P(None, None, "tensor")
    in_specs = (
        rows,
        P("shard"),
        P(None, "shard", None, "tensor"),
        by_column,
        P(None, "tensor", "shard"),
        P(None, "shard", "tensor"),
        P(None, "tensor"),
        P(None, "tensor", "shard"),
        P(),
        P(),
        P(),
        rows,
    )
    out_specs = (
        own_rows,
        own_rows,
        P(None, "shard", None, "tensor"),
        P(None, "tensor", "shard"),
        P(None, "shard", "tensor"),
        P(None, "tensor", "shard"),
        by_column,
        P(None, "tensor"),
        by_column,
        by_column,
        by_column,
    )
    return jax.shard_map(shards, mesh=mesh, in_specs=in_specs, out_specs=out_specs, check_vma=False)
```

```python
import functools

import jax
import jax.numpy as jnp
from jax import lax
from jax.experimental import pallas as pl
from jax.experimental.pallas import tpu as pltpu
from jax.sharding import PartitionSpec as P

HD = 64
HEADS = 4
BLK = 128
LEN = 2048
D = 1024
HALF = 512
COLS = 256
UNITS = 1024
RING = 16
EPSILON = 1e-05
NEGATIVE = -1e30
ROOT_HALF = 0.7071067811865476
DENSITY = 0.3989422804014327
BF = jnp.bfloat16
F32 = jnp.float32

NN = (((1,), (0,)), ((), ()))
NT = (((1,), (1,)), ((), ()))
TN = (((0,), (0,)), ((), ()))


def mm(a, b, dims=NN):
    return lax.dot_general(a, b, dims, preferred_element_type=F32)


def call(kernel, micros, outs, scalars, *args, scratch=(), vmem=20):
    specs = [pl.BlockSpec(memory_space=pltpu.SMEM)]
    specs += [pl.BlockSpec(memory_space=pltpu.VMEM)] * len(args)
    return pl.pallas_call(
        kernel,
        out_shape=[jax.ShapeDtypeStruct(shape, dtype) for shape, dtype in outs],
        in_specs=specs,
        out_specs=[pl.BlockSpec(memory_space=pltpu.VMEM)] * len(outs),
        scratch_shapes=list(scratch),
        compiler_params=pltpu.CompilerParams(vmem_limit_bytes=vmem << 20),
        cost_estimate=pl.CostEstimate(
            flops=int(micros * 1.1e9), bytes_accessed=int(micros * 3e6), transcendentals=0
        ),
    )(scalars, *args)


def half_at(shard, own):
    return pl.ds(pl.multiple_of((shard if own else 1 - shard) * HALF, HALF), HALF)


def by_head(rows):
    lane = lax.broadcasted_iota(jnp.int32, rows.shape, 1) // HD
    return jnp.concatenate(
        [jnp.where(lane == head, rows, jnp.zeros_like(rows)) for head in range(HEADS)], axis=0
    )


def norm_rows(summed, gain, shift):
    centred = summed - jnp.mean(summed, axis=-1, keepdims=True)
    factor = lax.rsqrt(jnp.mean(centred * centred, axis=-1, keepdims=True) + EPSILON)
    normed = centred * factor
    return normed * gain + shift, normed, factor


def norm_back(incoming, normed, factor, gain):
    scaled = incoming * gain
    centre = jnp.mean(scaled, axis=-1, keepdims=True)
    along = jnp.mean(scaled * normed, axis=-1, keepdims=True)
    return factor * (scaled - centre - normed * along)


def split_rows(place, rows_ref, mine_ref, theirs_ref):
    core = place[2]
    for part in range(2):
        mine = pl.multiple_of(part * 64 + core * 32, 32)
        theirs = pl.multiple_of(part * 64 + (1 - core) * 32, 32)
        mine_ref[pl.ds(part * 32, 32), :] = rows_ref[pl.ds(mine, 32), :].astype(BF)
        theirs_ref[pl.ds(part * 32, 32), :] = rows_ref[pl.ds(theirs, 32), :].astype(BF)


def both(mine, sibling, shard, own):
    cols = half_at(shard, own)
    return jnp.concatenate([mine[:, cols], sibling[:, cols]], axis=0)


def core_rows(place, ref):
    core = place[2]
    return jnp.concatenate(
        [ref[pl.ds(pl.multiple_of(part * 64 + core * 32, 32), 32), :] for part in range(2)], axis=0
    )


def attend_kernel(
    place, x_mine, x_sib, tokens, w_own, w_oth, b_qv, id_q, id_k, wo_own, wo_oth,
    q_ref, k_ref, v_ref, o_ref, ob_ref, lse_ref, mine_ref, theirs_ref, part_ref,
):
    shard, core = place[0], place[2]
    biases = b_qv[...].astype(F32)
    own, oth = half_at(shard, True), half_at(shard, False)

    @pl.loop(0, RING // 4)
    def _(step):
        blocks = pl.ds(step * 4, 4)
        for x, side in ((x_mine, core), (x_sib, 1 - core)):
            x_own = x[blocks, :, own].reshape(256, HALF)
            x_oth = x[blocks, :, oth].reshape(256, HALF)
            keys = mm(x_own, w_own[1]) + mm(x_oth, w_oth[1])
            values = mm(x_own, w_own[2]) + mm(x_oth, w_oth[2]) + biases[1:2]
            k_ref[blocks, side] = keys.astype(BF).reshape(4, 64, COLS)
            v_ref[blocks, side] = values.astype(BF).reshape(4, 64, COLS)

    keys, values = k_ref[...].reshape(LEN, COLS), v_ref[...].reshape(LEN, COLS)
    q = (mm(tokens[:, own], w_own[0]) + mm(tokens[:, oth], w_oth[0]) + biases[0:1]).astype(BF)
    q_ref[...] = q
    q_heads = by_head(q * BF(HD ** -0.5))
    allowed = id_k[place[1]] == jnp.concatenate(
        [id_q[index][:, 0:BLK] for index in range(RING)], axis=1
    )
    lane = lax.broadcasted_iota(jnp.int32, (BLK, COLS), 1) // HD
    out = jnp.zeros((BLK, COLS), F32)
    for head in range(HEADS):
        scores = mm(q_heads[head * BLK : (head + 1) * BLK], keys, NT)
        scores = jnp.where(allowed, scores, NEGATIVE)
        highest = jnp.max(scores, axis=-1, keepdims=True)
        weights = jnp.exp(scores - highest)
        total = jnp.sum(weights, axis=-1, keepdims=True)
        mixed = mm(weights.astype(BF), values) / total
        out = jnp.where(lane == head, mixed, out)
        column = jnp.broadcast_to(highest + jnp.log(total), (BLK, BLK))
        lse_ref[:, head * BLK : (head + 1) * BLK] = column.T[0:1, :]
    o_ref[...] = out
    low = out.astype(BF)
    ob_ref[...] = low
    part_ref[:, own] = mm(low, wo_own[...])
    part_ref[:, oth] = mm(low, wo_oth[...])
    split_rows(place, part_ref, mine_ref, theirs_ref)


def first_norm(summed, gain, shift):
    return norm_rows(summed, gain[0:1, :].astype(F32), shift[0:1, :].astype(F32))


def first_norm_kernel(place, tokens, chip, recv, extra, gain, shift, s_ref, hb_ref):
    branch = chip[...].astype(F32) + recv[...].astype(F32) + extra[0:1, :].astype(F32)
    s_ref[...] = core_rows(place, tokens).astype(F32) + branch
    hb_ref[...] = first_norm(s_ref[...], gain, shift)[0].astype(BF)


def other_up(other, side):
    return other[:, side * 32 : side * 32 + 32, :].reshape(HALF, HALF)


def other_down(other):
    return other[:, 64:128, :].reshape(UNITS, HALF)


def up_down_kernel(
    place, hb, hb_sib, up_own, down_own, other, b_up,
    ub_ref, slope_ref, mine_ref, theirs_ref, part_ref,
):
    shard = place[0]
    own, oth = both(hb, hb_sib, shard, True), both(hb, hb_sib, shard, False)
    for side in range(2):
        cols = pl.ds(side * HALF, HALF)
        before = mm(own, up_own[:, cols]) + mm(oth, other_up(other, side)) + b_up[:, cols].astype(F32)
        bell = 0.5 * (1.0 + lax.erf(before * ROOT_HALF))
        ub_ref[:, cols] = (before * bell).astype(BF)
        slope_ref[:, cols] = bell + before * DENSITY * jnp.exp(-0.5 * before * before)
    after = ub_ref[...]
    part_ref[:, half_at(shard, True)] = mm(after, down_own[...])
    part_ref[:, half_at(shard, False)] = mm(after, other_down(other))
    mine_ref[...] = part_ref[0:64, :].astype(BF)
    theirs_ref[...] = part_ref[64:128, :].astype(BF)


def second_norm_kernel(
    place, first, chip, recv, extra, gain, shift, cot, out_ref, dx_ref, dz_ref, sums_ref, keep
):
    far = place[3]
    middle = first_norm(first[...], gain, shift)[0]
    gains = gain[1:2, :].astype(F32)
    branch = chip[...].astype(F32) + recv[...].astype(F32) + extra[1:2, :].astype(F32)
    hidden, normed, factor = norm_rows(middle + branch, gains, shift[1:2, :].astype(F32))
    keep[...] = hidden
    out_ref[...] = keep[pl.ds(pl.multiple_of(far * 32, 32), 32), :]
    grad = core_rows(place, cot)
    back = norm_back(grad, normed, factor, gains)
    dx_ref[0:64, :] = back
    dx_ref[64:128, :] = first[...]
    low = back.astype(BF)
    dz_ref[...] = low
    sums_ref[0:1, :] = jnp.sum(low.astype(F32), axis=0, keepdims=True)
    sums_ref[1:2, :] = jnp.sum(grad * normed, axis=0, keepdims=True)
    sums_ref[2:3, :] = jnp.sum(grad, axis=0, keepdims=True)
    sums_ref[3:8, :] = jnp.zeros((5, D), F32)


def down_up_kernel(
    place, dz, dz_sib, slope, up_own, down_own, other, da_ref, mine_ref, theirs_ref, part_ref
):
    shard = place[0]
    own, oth = both(dz, dz_sib, shard, True), both(dz, dz_sib, shard, False)
    after = mm(own, down_own[...], NT) + mm(oth, other_down(other), NT)
    da_ref[...] = (after * slope[...]).astype(BF)
    before = da_ref[...]
    part_ref[:, half_at(shard, True)] = mm(before, up_own[...], NT)
    part_ref[:, half_at(shard, False)] = sum(
        mm(before[:, side * HALF : (side + 1) * HALF], other_up(other, side), NT) for side in range(2)
    )
    mine_ref[...] = part_ref[0:64, :].astype(BF)
    theirs_ref[...] = part_ref[64:128, :].astype(BF)


def unit_grads_kernel(
    place, hb, hb_sib, da, ub, dz, dz_sib, pair_ub, pair_late, pair_dz, pair_da, out_ref, bias_ref
):
    shard = place[0]
    rows = jnp.concatenate([both(hb, hb_sib, shard, True), pair_late[:, 0:512]], axis=0)
    units = jnp.concatenate([da[...], pair_da[...]], axis=0)
    pair_after = jnp.concatenate([pair_ub[...], pair_late[:, 512:1024]], axis=1)
    after = jnp.concatenate([ub[...], pair_after], axis=0)
    grads = jnp.concatenate([both(dz, dz_sib, shard, True), pair_dz[...]], axis=0)
    for part in range(4):
        cols = slice(part * COLS, (part + 1) * COLS)
        term = mm(rows, units[:, cols], TN).astype(BF)
        out_ref[:, part * 32 : part * 32 + 32, :] = term.reshape(RING, 32, COLS)
    for side in range(2):
        cols = slice(side * COLS, (side + 1) * COLS)
        term = mm(after, grads[:, cols], TN).astype(BF)
        out_ref[:, 128 + side * 64 : 192 + side * 64, :] = term.reshape(RING, 64, COLS)
    total = jnp.sum(units.astype(F32), axis=0, keepdims=True)
    bias_ref[...] = jnp.concatenate(
        [total[:, part * COLS : (part + 1) * COLS] for part in range(4)]
        + [jnp.zeros((4, COLS), F32)],
        axis=0,
    )


def first_back_kernel(
    place, dx, chip, recv, gain, shift, sums_in, d_ref, low_ref, sums_ref, keep
):
    far = place[3]
    _, normed, factor = first_norm(dx[64:128, :], gain, shift)
    grad = dx[0:64, :] + (chip[...].astype(F32) + recv[...].astype(F32))
    back = norm_back(grad, normed, factor, gain[0:1, :].astype(F32))
    keep[...] = back
    d_ref[...] = keep[pl.ds(pl.multiple_of(far * 32, 32), 32), :]
    low = back.astype(BF)
    low_ref[...] = low
    sums_ref[...] = sums_in[...]
    sums_ref[3:4, :] = jnp.sum(low.astype(F32), axis=0, keepdims=True)
    sums_ref[4:5, :] = jnp.sum(grad * normed, axis=0, keepdims=True)
    sums_ref[5:6, :] = jnp.sum(grad, axis=0, keepdims=True)


def parts(row):
    high = row.astype(BF)
    rest = row - high.astype(F32)
    middle = rest.astype(BF)
    return (high, middle, (rest - middle.astype(F32)).astype(BF))


def out_back_kernel(
    place, low, low_sib, o, lse, wo_own, wo_oth, own_ref, oth_ref, d_ref, delta_ref, pack_ref, nat_ref
):
    shard = place[0]
    core = place[2]
    for part in range(2):
        for rows, side in ((low, core), (low_sib, 1 - core)):
            at = pl.ds(pl.multiple_of(part * 64 + side * 32, 32), 32)
            nat_ref[at, :] = rows[part * 32 : part * 32 + 32, :]
    own, oth = nat_ref[:, half_at(shard, True)], nat_ref[:, half_at(shard, False)]
    own_ref[...] = own
    oth_ref[...] = oth
    d_out = (mm(own, wo_own[...], NT) + mm(oth, wo_oth[...], NT)).astype(BF)
    d_ref[...] = d_out
    turned = (d_out.astype(F32) * o[...]).T
    delta = jnp.concatenate(
        [
            jnp.sum(turned[head * HD : (head + 1) * HD], axis=0, keepdims=True)
            for head in range(HEADS)
        ],
        axis=1,
    )
    delta_ref[...] = delta
    rows = [d_out]
    for row in parts(lse[...]) + parts(delta):
        rows += [row[:, 0:COLS], row[:, COLS : 2 * COLS]]
    rows.append(jnp.zeros((4, COLS), BF))
    packed = jnp.concatenate(rows, axis=0)
    for index in range(RING):
        pack_ref[index] = packed


def query_grad_kernel(place, q, k, v, d_out, lse, delta, id_q, id_k, dq_ref, acc_ref):
    q_heads = by_head(q[...] * BF(HD ** -0.5))
    d_heads = by_head(d_out[...])
    acc_ref[...] = jnp.zeros_like(acc_ref)

    @pl.loop(0, RING // 2)
    def _(step):
        blocks = pl.ds(step * 2, 2)
        keys, values = k[blocks].reshape(256, COLS), v[blocks].reshape(256, COLS)
        allowed = id_k[blocks].reshape(256, 1) == id_q[place[1]]
        probs = jnp.where(allowed, jnp.exp(mm(keys, q_heads, NT) - lse[...]), 0.0)
        d_scores = (probs * (mm(values, d_heads, NT) - delta[...])).astype(BF)
        acc_ref[...] += mm(d_scores, keys, TN)

    lane = lax.broadcasted_iota(jnp.int32, (BLK, COLS), 1) // HD
    total = jnp.zeros((BLK, COLS), F32)
    for head in range(HEADS):
        total = jnp.where(lane == head, acc_ref[head * BLK : (head + 1) * BLK, :], total)
    dq_ref[...] = (total * HD ** -0.5).astype(BF)


def key_grad_kernel(
    place, x_mine, x_sib, b_qv, k, v, dq, recv, ids, id_k, w_own, w_oth,
    d_ref, mine_ref, theirs_ref, part_ref, q,
):
    shard, block, core = place[0], place[1], place[2]
    bias = b_qv[0:1, :].astype(F32)

    @pl.loop(0, RING // 4)
    def _(step):
        blocks = pl.ds(step * 4, 4)
        for x, side in ((x_mine, core), (x_sib, 1 - core)):
            queries = (
                mm(x[blocks, :, half_at(shard, True)].reshape(256, HALF), w_own[0])
                + mm(x[blocks, :, half_at(shard, False)].reshape(256, HALF), w_oth[0])
                + bias
            )
            q[blocks, side] = queries.astype(BF).reshape(4, 64, COLS)

    keys, values = k[block].reshape(BLK, COLS), v[block].reshape(BLK, COLS)
    own_ids = id_k[block]

    def step(index, carry):
        d_key, d_value = carry
        q_heads = by_head(q[index].reshape(BLK, COLS) * BF(HD ** -0.5))
        d_heads = by_head(recv[index, 0:BLK, :])
        tail = recv[index, BLK : BLK + 16, :].astype(F32)
        rows = [
            jnp.concatenate(
                [tail[at + side : at + side + 1] + tail[at + 2 + side : at + 3 + side]
                 + tail[at + 4 + side : at + 5 + side] for side in range(2)],
                axis=1,
            )
            for at in (0, 6)
        ]
        allowed = own_ids == ids[index]
        probs = jnp.where(allowed, jnp.exp(mm(keys, q_heads, NT) - rows[0]), 0.0)
        d_scores = (probs * (mm(values, d_heads, NT) - rows[1])).astype(BF)
        return d_key + mm(d_scores, q_heads), d_value + mm(probs.astype(BF), d_heads)

    start = jnp.zeros((BLK, COLS), F32)
    d_key, d_value = lax.fori_loop(0, RING, step, (start, start), unroll=2)
    d_ref[:, 0:COLS] = dq[...]
    d_ref[:, COLS : 2 * COLS] = d_key.astype(BF)
    d_ref[:, 2 * COLS : 3 * COLS] = d_value.astype(BF)
    for own, weight in ((True, w_own), (False, w_oth)):
        part_ref[:, half_at(shard, own)] = (
            mm(d_ref[:, 0:COLS], weight[0], NT)
            + mm(d_ref[:, COLS : 2 * COLS], weight[1], NT)
            + mm(d_ref[:, 2 * COLS : 3 * COLS], weight[2], NT)
        )
    split_rows(place, part_ref, mine_ref, theirs_ref)


def ring_sum(recv, rows):
    total = recv[0, rows, :].astype(F32)
    for index in range(1, RING):
        total = total + recv[index, rows, :].astype(F32)
    return total


def in_grads_kernel(
    place, tokens, d, d_pair, pair_in, ob, low, low_pair, sums, unit_sums, out_ref
):
    shard = place[0]
    rows = jnp.concatenate([tokens[:, half_at(shard, True)], pair_in[:, 256:768]], axis=0)
    grads = jnp.concatenate([d[...], d_pair[...]], axis=0)
    for part in range(3):
        term = mm(rows, grads[:, part * COLS : (part + 1) * COLS], TN).astype(BF)
        out_ref[:, part * 32 : part * 32 + 32, :] = term.reshape(RING, 32, COLS)
    heads = jnp.concatenate([ob[...], pair_in[:, 0:256]], axis=0)
    outs = jnp.concatenate([low[...], low_pair[...]], axis=0)
    for side in range(2):
        term = mm(heads, outs[:, side * COLS : (side + 1) * COLS], TN).astype(BF)
        out_ref[:, 96 + side * 16 : 112 + side * 16, :] = term.reshape(RING, 16, COLS)
    wide = grads.astype(F32)
    small = jnp.concatenate(
        [
            sums[0:6, :],
            jnp.sum(wide[:, 0:COLS], axis=0, keepdims=True),
            jnp.sum(wide[:, 2 * COLS : 3 * COLS], axis=0, keepdims=True),
            unit_sums[...],
        ],
        axis=0,
    ).astype(BF)
    for index in range(RING):
        out_ref[index, 128:144, :] = small


def unit_total_kernel(place, recv, low_ref):
    low_ref[...] = ring_sum(recv, slice(0, 256)).astype(BF)


def total_kernel(place, recv, small_ref, out_ref):
    total = ring_sum(recv, slice(0, 144))
    small_ref[...] = total[128:144]
    low = total[0:128].astype(BF)
    for index in range(RING):
        out_ref[index] = low


def unpack_units_kernel(place, recv, up_ref, down_ref):
    for part in range(4):
        up_ref[:, part * COLS : (part + 1) * COLS] = (
            recv[:, part * 32 : part * 32 + 32, :].reshape(HALF, COLS).astype(F32)
        )
    for side in range(2):
        down_ref[:, side * COLS : (side + 1) * COLS] = (
            recv[:, 128 + side * 64 : 192 + side * 64, :].reshape(UNITS, COLS).astype(F32)
        )


def unpack_kernel(place, recv, in_ref, out_ref):
    for part in range(3):
        in_ref[part] = recv[:, part * 32 : part * 32 + 32, :].reshape(HALF, COLS).astype(F32)
    for side in range(2):
        out_ref[:, side * COLS : (side + 1) * COLS] = (
            recv[:, 96 + side * 16 : 112 + side * 16, :].reshape(COLS, COLS).astype(F32)
        )


def swap(value, axis, bit):
    size = lax.axis_size(axis)
    return lax.ppermute(value, axis, [(index, index ^ bit) for index in range(size)])


def tensor_sum(mine, theirs):
    chip = (mine.astype(F32) + swap(theirs, "tensor", 1).astype(F32)).astype(BF)
    return chip, swap(chip, "tensor", 2)


def shards(
    tokens, segment_ids, w_qkv, b_qv, w_out, w_up, b_up, w_down, out_bias, ln_gain, ln_bias, cotangent
):
    shard, block, tensor = (lax.axis_index(name) for name in ("shard", "context", "tensor"))
    core, far = tensor % 2, tensor // 2
    place = jnp.stack([shard, block, core, far]).astype(jnp.int32)
    w_in = jnp.transpose(w_qkv[0], (1, 0, 2))
    w_out, w_up, w_down = w_out[0], w_up[0], w_down[0]
    extra, gain, shift = out_bias[0], ln_gain[0], ln_bias[0]
    together = lax.optimization_barrier

    up_rows = lax.dynamic_slice_in_dim(w_up, block * 32, 32, 0)
    down_rows = lax.dynamic_slice_in_dim(w_down, block * 64, 64, 0)
    unit_rows = swap(
        jnp.concatenate([up_rows[:, :HALF], up_rows[:, HALF:], down_rows], axis=0), "shard", 1
    )
    other = lax.all_gather(unit_rows, "context", axis=0)
    w_in_late, _ = together((w_in, unit_rows))
    in_oth = swap(w_in_late, "shard", 1)
    out_oth = swap(w_out, "shard", 1)

    spread = jnp.broadcast_to(
        jnp.where(core == 0, tokens[0:64], tokens[64:128])[None], (RING, 64, D)
    )
    x_mine = lax.all_to_all(spread, "context", 0, 0, tiled=True)
    x_mine, in_oth, out_oth = together((x_mine, in_oth, out_oth))
    x_sib = swap(x_mine, "tensor", 1)

    id_column = segment_ids.reshape(RING, BLK, 1)
    id_heads = jnp.tile(segment_ids.reshape(RING, 1, BLK), (1, 1, HEADS))
    all_heads = ((RING, 2, 64, COLS), BF)
    halves = [((64, D), BF), ((64, D), BF)]
    whole = pltpu.VMEM((BLK, D), F32)
    q, k, v, o, ob, lse, mine, theirs = call(
        attend_kernel, 10,
        [((BLK, COLS), BF)] + [all_heads] * 2 + [((BLK, COLS), F32), ((BLK, COLS), BF), ((1, HEADS * BLK), F32)] + halves,
        place, x_mine, x_sib, tokens, w_in, in_oth, b_qv[0], id_heads, id_column,
        w_out, out_oth,
        scratch=[whole], vmem=60,
    )
    chip, recv = tensor_sum(mine, theirs)
    first, low_mid = call(
        first_norm_kernel, 1, [((64, D), F32), ((64, D), BF)],
        place, tokens, chip, recv, extra, gain, shift,
    )
    hb_sib = swap(low_mid, "tensor", 1)
    ub, slope, mine, theirs = call(
        up_down_kernel, 2, [((BLK, UNITS), BF), ((BLK, UNITS), F32)] + halves,
        place, low_mid, hb_sib, w_up, w_down, other, b_up,
        scratch=[whole],
    )
    away = (1 - shard) * HALF

    def away_half(mine, sibling):
        rows = [lax.dynamic_slice_in_dim(half, away, HALF, 1) for half in (mine, sibling)]
        return jnp.concatenate(rows, axis=0)

    pair_in = swap(
        jnp.concatenate([ob, lax.dynamic_slice_in_dim(tokens, away, HALF, 1)], axis=1), "shard", 1
    )
    pair_ub = swap(ub[:, 0:HALF], "shard", 1)
    pair_late = swap(
        jnp.concatenate([away_half(low_mid, hb_sib), ub[:, HALF:UNITS]], axis=1), "shard", 1
    )
    chip, recv = tensor_sum(mine, theirs)
    hidden_out, dx, low_second, sums = call(
        second_norm_kernel, 2,
        [((32, D), F32), ((BLK, D), F32), ((64, D), BF), ((8, D), F32)],
        place, first, chip, recv, extra, gain, shift, cotangent,
        scratch=[pltpu.VMEM((64, D), F32)],
    )
    dz_sib = swap(low_second, "tensor", 1)
    dz_sib, pair_ub = together((dz_sib, pair_ub))
    pair_dz = swap(away_half(low_second, dz_sib), "shard", 1)
    da, mine, theirs = call(
        down_up_kernel, 2, [((BLK, UNITS), BF)] + halves,
        place, low_second, dz_sib, slope, w_up, w_down, other,
        scratch=[whole],
    )
    pair_da = swap(da, "shard", 1)
    chip, recv = tensor_sum(mine, theirs)
    d_first, low_first, sums = call(
        first_back_kernel, 1.5,
        [((32, D), F32), ((64, D), BF), ((8, D), F32)],
        place, dx, chip, recv, gain, shift, sums,
        scratch=[pltpu.VMEM((64, D), F32)],
    )
    low_sib = swap(low_first, "tensor", 1)
    low_own, low_oth, d_out, delta, packed = call(
        out_back_kernel, 1.5,
        [
            ((BLK, HALF), BF), ((BLK, HALF), BF), ((BLK, COLS), BF), ((1, HEADS * BLK), F32),
            ((RING, 144, COLS), BF),
        ],
        place, low_first, low_sib, o, lse, w_out, out_oth,
        scratch=[pltpu.VMEM((BLK, D), BF)], vmem=60,
    )
    packs = lax.all_to_all(packed, "context", 0, 0, tiled=True)
    (dq,) = call(
        query_grad_kernel, 5, [((BLK, COLS), BF)],
        place, q, k, v, d_out, lse, delta, id_heads, id_column,
        scratch=[pltpu.VMEM((HEADS * BLK, COLS), F32)], vmem=60,
    )
    low_mid, dq = together((low_mid, dq))
    unit_grads, unit_small = call(
        unit_grads_kernel, 3, [((RING, 256, COLS), BF), ((8, COLS), F32)],
        place, low_mid, hb_sib, da, ub, low_second, dz_sib, pair_ub, pair_late, pair_dz, pair_da,
    )
    packs, unit_grads, dq = together((packs, unit_grads, dq))
    unit_recv = lax.all_to_all(unit_grads, "context", 0, 0, tiled=True)
    low_pair = swap(low_oth, "shard", 1)
    sums = sums + swap(sums, "tensor", 1)
    sums = lax.dynamic_slice_in_dim(sums, tensor * COLS, COLS, 1)
    sums = sums + swap(sums, "shard", 1)
    d_mixed, mine, theirs = call(
        key_grad_kernel, 6, [((BLK, 3 * COLS), BF)] + halves,
        place, x_mine, x_sib, b_qv[0], k, v, dq, packs, id_heads, id_column, w_in, in_oth,
        scratch=[whole, pltpu.VMEM((RING, 2, 64, COLS), BF)], vmem=60,
    )
    d_pair = swap(d_mixed, "shard", 1)
    chip = mine.astype(F32) + swap(theirs, "tensor", 1).astype(F32)
    chip_far = lax.dynamic_slice_in_dim(chip, (1 - far) * 32, 32, 0).astype(BF)
    chip_near = lax.dynamic_slice_in_dim(chip, far * 32, 32, 0)
    grad_tokens = d_first + (chip_near + swap(chip_far, "tensor", 2).astype(F32))
    (in_grads,) = call(
        in_grads_kernel, 2.5, [((RING, 144, COLS), BF)],
        place, tokens, d_mixed, d_pair, pair_in, ob, low_own, low_pair, sums, unit_small,
    )
    in_grads, unit_recv = together((in_grads, unit_recv))
    recv = lax.all_to_all(in_grads, "context", 0, 0, tiled=True)
    (unit_total,) = call(unit_total_kernel, 1, [((COLS, COLS), BF)], place, unit_recv)
    unit_all = lax.all_gather(unit_total, "context", axis=0)
    recv, _ = together((recv, unit_total))
    small, totals = call(
        total_kernel, 2, [((16, COLS), F32), ((RING, 128, COLS), BF)], place, recv
    )
    recv = lax.all_to_all(totals, "context", 0, 0, tiled=True)
    grad_in, grad_w_out = call(
        unpack_kernel, 2, [((3, HALF, COLS), F32), ((COLS, HALF), F32)], place, recv
    )
    grad_w_up, grad_w_down = call(
        unpack_units_kernel, 2, [((HALF, UNITS), F32), ((UNITS, HALF), F32)],
        place, unit_all, vmem=60,
    )
    return (
        hidden_out,
        grad_tokens,
        jnp.transpose(grad_in, (1, 0, 2))[None],
        grad_w_out[None],
        grad_w_up[None],
        grad_w_down[None],
        small[6:8][None],
        small[8:12].reshape(1, UNITS),
        jnp.stack([small[3], small[0]])[None],
        jnp.stack([small[4], small[1]])[None],
        jnp.stack([small[5], small[2]])[None],
    )


def solution(mesh):
    rows = P(("shard", "context"), None)
    own_rows = P(("shard", "context", "tensor"), None)
    by_column = P(None, None, "tensor")
    in_specs = (
        rows,
        P("shard"),
        P(None, "shard", None, "tensor"),
        by_column,
        P(None, "tensor", "shard"),
        P(None, "shard", "tensor"),
        P(None, "tensor"),
        P(None, "tensor", "shard"),
        P(),
        P(),
        P(),
        rows,
    )
    out_specs = (
        own_rows,
        own_rows,
        P(None, "shard", None, "tensor"),
        P(None, "tensor", "shard"),
        P(None, "shard", "tensor"),
        P(None, "tensor", "shard"),
        by_column,
        P(None, "tensor"),
        by_column,
        by_column,
        by_column,
    )
    return jax.shard_map(shards, mesh=mesh, in_specs=in_specs, out_specs=out_specs, check_vma=False)
```

```python
import functools

import jax
import jax.numpy as jnp
from jax import lax
from jax.experimental import pallas as pl
from jax.experimental.pallas import tpu as pltpu
from jax.sharding import PartitionSpec as P

HD = 64
HEADS = 4
BLK = 128
LEN = 2048
D = 1024
HALF = 512
COLS = 256
UNITS = 1024
RING = 16
EARLY = 768
EPSILON = 1e-05
NEGATIVE = -1e30
ROOT_HALF = 0.7071067811865476
DENSITY = 0.3989422804014327
BF = jnp.bfloat16
F32 = jnp.float32

NN = (((1,), (0,)), ((), ()))
NT = (((1,), (1,)), ((), ()))
TN = (((0,), (0,)), ((), ()))


def mm(a, b, dims=NN):
    return lax.dot_general(a, b, dims, preferred_element_type=F32)


def call(kernel, micros, outs, scalars, *args, scratch=(), vmem=20):
    specs = [pl.BlockSpec(memory_space=pltpu.SMEM)]
    specs += [pl.BlockSpec(memory_space=pltpu.VMEM)] * len(args)
    return pl.pallas_call(
        kernel,
        out_shape=[jax.ShapeDtypeStruct(shape, dtype) for shape, dtype in outs],
        in_specs=specs,
        out_specs=[pl.BlockSpec(memory_space=pltpu.VMEM)] * len(outs),
        scratch_shapes=list(scratch),
        compiler_params=pltpu.CompilerParams(vmem_limit_bytes=vmem << 20),
        cost_estimate=pl.CostEstimate(
            flops=int(micros * 1.1e9), bytes_accessed=int(micros * 3e6), transcendentals=0
        ),
    )(scalars, *args)


def half_at(shard, own):
    return pl.ds(pl.multiple_of((shard if own else 1 - shard) * HALF, HALF), HALF)


def by_head(rows):
    lane = lax.broadcasted_iota(jnp.int32, rows.shape, 1) // HD
    return jnp.concatenate(
        [jnp.where(lane == head, rows, jnp.zeros_like(rows)) for head in range(HEADS)], axis=0
    )


def norm_rows(summed, gain, shift):
    centred = summed - jnp.mean(summed, axis=-1, keepdims=True)
    factor = lax.rsqrt(jnp.mean(centred * centred, axis=-1, keepdims=True) + EPSILON)
    normed = centred * factor
    return normed * gain + shift, normed, factor


def norm_back(incoming, normed, factor, gain):
    scaled = incoming * gain
    centre = jnp.mean(scaled, axis=-1, keepdims=True)
    along = jnp.mean(scaled * normed, axis=-1, keepdims=True)
    return factor * (scaled - centre - normed * along)


def split_rows(place, rows_ref, mine_ref, theirs_ref):
    core = place[2]
    for part in range(2):
        mine = pl.multiple_of(part * 64 + core * 32, 32)
        theirs = pl.multiple_of(part * 64 + (1 - core) * 32, 32)
        mine_ref[pl.ds(part * 32, 32), :] = rows_ref[pl.ds(mine, 32), :].astype(BF)
        theirs_ref[pl.ds(part * 32, 32), :] = rows_ref[pl.ds(theirs, 32), :].astype(BF)


def both(mine, sibling, shard, own):
    cols = half_at(shard, own)
    return jnp.concatenate([mine[:, cols], sibling[:, cols]], axis=0)


def core_rows(place, ref):
    core = place[2]
    return jnp.concatenate(
        [ref[pl.ds(pl.multiple_of(part * 64 + core * 32, 32), 32), :] for part in range(2)], axis=0
    )


def attend_kernel(
    place, x_mine, x_sib, tokens, w_own, w_oth, b_qv, id_q, id_k, wo_own, wo_oth,
    q_ref, k_ref, v_ref, o_ref, ob_ref, lse_ref, mine_ref, theirs_ref, part_ref,
):
    shard, core = place[0], place[2]
    biases = b_qv[...].astype(F32)
    own, oth = half_at(shard, True), half_at(shard, False)

    @pl.loop(0, RING // 4)
    def _(step):
        blocks = pl.ds(step * 4, 4)
        for x, side in ((x_mine, core), (x_sib, 1 - core)):
            x_own = x[blocks, :, own].reshape(256, HALF)
            x_oth = x[blocks, :, oth].reshape(256, HALF)
            keys = mm(x_own, w_own[1]) + mm(x_oth, w_oth[1])
            values = mm(x_own, w_own[2]) + mm(x_oth, w_oth[2]) + biases[1:2]
            k_ref[blocks, side] = keys.astype(BF).reshape(4, 64, COLS)
            v_ref[blocks, side] = values.astype(BF).reshape(4, 64, COLS)

    keys, values = k_ref[...].reshape(LEN, COLS), v_ref[...].reshape(LEN, COLS)
    q = (mm(tokens[:, own], w_own[0]) + mm(tokens[:, oth], w_oth[0]) + biases[0:1]).astype(BF)
    q_ref[...] = q
    q_heads = by_head(q * BF(HD ** -0.5))
    allowed = id_k[place[1]] == jnp.concatenate(
        [id_q[index][:, 0:BLK] for index in range(RING)], axis=1
    )
    lane = lax.broadcasted_iota(jnp.int32, (BLK, COLS), 1) // HD
    out = jnp.zeros((BLK, COLS), F32)
    for head in range(HEADS):
        scores = mm(q_heads[head * BLK : (head + 1) * BLK], keys, NT)
        scores = jnp.where(allowed, scores, NEGATIVE)
        highest = jnp.max(scores, axis=-1, keepdims=True)
        weights = jnp.exp(scores - highest)
        total = jnp.sum(weights, axis=-1, keepdims=True)
        mixed = mm(weights.astype(BF), values) / total
        out = jnp.where(lane == head, mixed, out)
        column = jnp.broadcast_to(highest + jnp.log(total), (BLK, BLK))
        lse_ref[:, head * BLK : (head + 1) * BLK] = column.T[0:1, :]
    o_ref[...] = out
    low = out.astype(BF)
    ob_ref[...] = low
    part_ref[:, own] = mm(low, wo_own[...])
    part_ref[:, oth] = mm(low, wo_oth[...])
    split_rows(place, part_ref, mine_ref, theirs_ref)


def first_norm(summed, gain, shift):
    return norm_rows(summed, gain[0:1, :].astype(F32), shift[0:1, :].astype(F32))


def first_norm_kernel(place, tokens, chip, recv, extra, gain, shift, s_ref, hb_ref):
    branch = chip[...].astype(F32) + recv[...].astype(F32) + extra[0:1, :].astype(F32)
    s_ref[...] = core_rows(place, tokens).astype(F32) + branch
    hb_ref[...] = first_norm(s_ref[...], gain, shift)[0].astype(BF)


def other_up(other, side):
    return other[:, side * 32 : side * 32 + 32, :].reshape(HALF, HALF)


def other_down(other):
    return other[:, 64:128, :].reshape(UNITS, HALF)


def up_down_kernel(
    place, hb, hb_sib, up_own, down_own, other, b_up,
    ub_ref, slope_ref, mine_ref, theirs_ref, part_ref,
):
    shard = place[0]
    own, oth = both(hb, hb_sib, shard, True), both(hb, hb_sib, shard, False)
    for side in range(2):
        cols = pl.ds(side * HALF, HALF)
        before = mm(own, up_own[:, cols]) + mm(oth, other_up(other, side)) + b_up[:, cols].astype(F32)
        bell = 0.5 * (1.0 + lax.erf(before * ROOT_HALF))
        ub_ref[:, cols] = (before * bell).astype(BF)
        slope_ref[:, cols] = bell + before * DENSITY * jnp.exp(-0.5 * before * before)
    after = ub_ref[...]
    part_ref[:, half_at(shard, True)] = mm(after, down_own[...])
    part_ref[:, half_at(shard, False)] = mm(after, other_down(other))
    mine_ref[...] = part_ref[0:64, :].astype(BF)
    theirs_ref[...] = part_ref[64:128, :].astype(BF)


def second_norm_kernel(
    place, first, chip, recv, extra, gain, shift, cot, out_ref, dx_ref, dz_ref, sums_ref, keep
):
    far = place[3]
    middle = first_norm(first[...], gain, shift)[0]
    gains = gain[1:2, :].astype(F32)
    branch = chip[...].astype(F32) + recv[...].astype(F32) + extra[1:2, :].astype(F32)
    hidden, normed, factor = norm_rows(middle + branch, gains, shift[1:2, :].astype(F32))
    keep[...] = hidden
    out_ref[...] = keep[pl.ds(pl.multiple_of(far * 32, 32), 32), :]
    grad = core_rows(place, cot)
    back = norm_back(grad, normed, factor, gains)
    dx_ref[0:64, :] = back
    dx_ref[64:128, :] = first[...]
    low = back.astype(BF)
    dz_ref[...] = low
    sums_ref[0:1, :] = jnp.sum(low.astype(F32), axis=0, keepdims=True)
    sums_ref[1:2, :] = jnp.sum(grad * normed, axis=0, keepdims=True)
    sums_ref[2:3, :] = jnp.sum(grad, axis=0, keepdims=True)
    sums_ref[3:8, :] = jnp.zeros((5, D), F32)


def down_up_kernel(
    place, dz, dz_sib, slope, up_own, down_own, other, da_ref, mine_ref, theirs_ref, part_ref
):
    shard = place[0]
    own, oth = both(dz, dz_sib, shard, True), both(dz, dz_sib, shard, False)
    after = mm(own, down_own[...], NT) + mm(oth, other_down(other), NT)
    da_ref[...] = (after * slope[...]).astype(BF)
    before = da_ref[...]
    part_ref[:, half_at(shard, True)] = mm(before, up_own[...], NT)
    part_ref[:, half_at(shard, False)] = sum(
        mm(before[:, side * HALF : (side + 1) * HALF], other_up(other, side), NT) for side in range(2)
    )
    mine_ref[...] = part_ref[0:64, :].astype(BF)
    theirs_ref[...] = part_ref[64:128, :].astype(BF)


def unit_grads_kernel(
    place, hb, hb_sib, da, ub, dz, dz_sib, pair_ub, pair_late, pair_dz, pair_da, out_ref, bias_ref
):
    shard = place[0]
    rows = jnp.concatenate([both(hb, hb_sib, shard, True), pair_late[:, 0:512]], axis=0)
    units = jnp.concatenate([da[...], pair_da[...]], axis=0)
    pair_after = jnp.concatenate([pair_ub[...], pair_late[:, HALF : HALF + UNITS - EARLY]], axis=1)
    after = jnp.concatenate([ub[...], pair_after], axis=0)
    grads = jnp.concatenate([both(dz, dz_sib, shard, True), pair_dz[...]], axis=0)
    for part in range(4):
        cols = slice(part * COLS, (part + 1) * COLS)
        term = mm(rows, units[:, cols], TN).astype(BF)
        out_ref[:, part * 32 : part * 32 + 32, :] = term.reshape(RING, 32, COLS)
    for side in range(2):
        cols = slice(side * COLS, (side + 1) * COLS)
        term = mm(after, grads[:, cols], TN).astype(BF)
        out_ref[:, 128 + side * 64 : 192 + side * 64, :] = term.reshape(RING, 64, COLS)
    total = jnp.sum(units.astype(F32), axis=0, keepdims=True)
    bias_ref[...] = jnp.concatenate(
        [total[:, part * COLS : (part + 1) * COLS] for part in range(4)]
        + [jnp.zeros((4, COLS), F32)],
        axis=0,
    )


def first_back_kernel(
    place, dx, chip, recv, gain, shift, sums_in, d_ref, low_ref, sums_ref, keep
):
    far = place[3]
    _, normed, factor = first_norm(dx[64:128, :], gain, shift)
    grad = dx[0:64, :] + (chip[...].astype(F32) + recv[...].astype(F32))
    back = norm_back(grad, normed, factor, gain[0:1, :].astype(F32))
    keep[...] = back
    d_ref[...] = keep[pl.ds(pl.multiple_of(far * 32, 32), 32), :]
    low = back.astype(BF)
    low_ref[...] = low
    sums_ref[...] = sums_in[...]
    sums_ref[3:4, :] = jnp.sum(low.astype(F32), axis=0, keepdims=True)
    sums_ref[4:5, :] = jnp.sum(grad * normed, axis=0, keepdims=True)
    sums_ref[5:6, :] = jnp.sum(grad, axis=0, keepdims=True)


def parts(row):
    high = row.astype(BF)
    rest = row - high.astype(F32)
    middle = rest.astype(BF)
    return (high, middle, (rest - middle.astype(F32)).astype(BF))


def out_back_kernel(
    place, low, low_sib, o, lse, wo_own, wo_oth, own_ref, oth_ref, d_ref, delta_ref, pack_ref, nat_ref
):
    shard = place[0]
    core = place[2]
    for part in range(2):
        for rows, side in ((low, core), (low_sib, 1 - core)):
            at = pl.ds(pl.multiple_of(part * 64 + side * 32, 32), 32)
            nat_ref[at, :] = rows[part * 32 : part * 32 + 32, :]
    own, oth = nat_ref[:, half_at(shard, True)], nat_ref[:, half_at(shard, False)]
    own_ref[...] = own
    oth_ref[...] = oth
    d_out = (mm(own, wo_own[...], NT) + mm(oth, wo_oth[...], NT)).astype(BF)
    d_ref[...] = d_out
    turned = (d_out.astype(F32) * o[...]).T
    delta = jnp.concatenate(
        [
            jnp.sum(turned[head * HD : (head + 1) * HD], axis=0, keepdims=True)
            for head in range(HEADS)
        ],
        axis=1,
    )
    delta_ref[...] = delta
    rows = [d_out]
    for row in parts(lse[...]) + parts(delta):
        rows += [row[:, 0:COLS], row[:, COLS : 2 * COLS]]
    rows.append(jnp.zeros((4, COLS), BF))
    packed = jnp.concatenate(rows, axis=0)
    for index in range(RING):
        pack_ref[index] = packed


def query_grad_kernel(place, q, k, v, d_out, lse, delta, id_q, id_k, dq_ref, acc_ref):
    q_heads = by_head(q[...] * BF(HD ** -0.5))
    d_heads = by_head(d_out[...])
    acc_ref[...] = jnp.zeros_like(acc_ref)

    @pl.loop(0, RING // 2)
    def _(step):
        blocks = pl.ds(step * 2, 2)
        keys, values = k[blocks].reshape(256, COLS), v[blocks].reshape(256, COLS)
        allowed = id_k[blocks].reshape(256, 1) == id_q[place[1]]
        probs = jnp.where(allowed, jnp.exp(mm(keys, q_heads, NT) - lse[...]), 0.0)
        d_scores = (probs * (mm(values, d_heads, NT) - delta[...])).astype(BF)
        acc_ref[...] += mm(d_scores, keys, TN)

    lane = lax.broadcasted_iota(jnp.int32, (BLK, COLS), 1) // HD
    total = jnp.zeros((BLK, COLS), F32)
    for head in range(HEADS):
        total = jnp.where(lane == head, acc_ref[head * BLK : (head + 1) * BLK, :], total)
    dq_ref[...] = (total * HD ** -0.5).astype(BF)


def key_grad_kernel(
    place, x_mine, x_sib, b_qv, k, v, dq, recv, ids, id_k, w_own, w_oth,
    d_ref, mine_ref, theirs_ref, part_ref, q,
):
    shard, block, core = place[0], place[1], place[2]
    bias = b_qv[0:1, :].astype(F32)

    @pl.loop(0, RING // 4)
    def _(step):
        blocks = pl.ds(step * 4, 4)
        for x, side in ((x_mine, core), (x_sib, 1 - core)):
            queries = (
                mm(x[blocks, :, half_at(shard, True)].reshape(256, HALF), w_own[0])
                + mm(x[blocks, :, half_at(shard, False)].reshape(256, HALF), w_oth[0])
                + bias
            )
            q[blocks, side] = queries.astype(BF).reshape(4, 64, COLS)

    keys, values = k[block].reshape(BLK, COLS), v[block].reshape(BLK, COLS)
    own_ids = id_k[block]

    def step(index, carry):
        d_key, d_value = carry
        q_heads = by_head(q[index].reshape(BLK, COLS) * BF(HD ** -0.5))
        d_heads = by_head(recv[index, 0:BLK, :])
        tail = recv[index, BLK : BLK + 16, :].astype(F32)
        rows = [
            jnp.concatenate(
                [tail[at + side : at + side + 1] + tail[at + 2 + side : at + 3 + side]
                 + tail[at + 4 + side : at + 5 + side] for side in range(2)],
                axis=1,
            )
            for at in (0, 6)
        ]
        allowed = own_ids == ids[index]
        probs = jnp.where(allowed, jnp.exp(mm(keys, q_heads, NT) - rows[0]), 0.0)
        d_scores = (probs * (mm(values, d_heads, NT) - rows[1])).astype(BF)
        return d_key + mm(d_scores, q_heads), d_value + mm(probs.astype(BF), d_heads)

    start = jnp.zeros((BLK, COLS), F32)
    d_key, d_value = lax.fori_loop(0, RING, step, (start, start), unroll=2)
    d_ref[:, 0:COLS] = dq[...]
    d_ref[:, COLS : 2 * COLS] = d_key.astype(BF)
    d_ref[:, 2 * COLS : 3 * COLS] = d_value.astype(BF)
    for own, weight in ((True, w_own), (False, w_oth)):
        part_ref[:, half_at(shard, own)] = (
            mm(d_ref[:, 0:COLS], weight[0], NT)
            + mm(d_ref[:, COLS : 2 * COLS], weight[1], NT)
            + mm(d_ref[:, 2 * COLS : 3 * COLS], weight[2], NT)
        )
    split_rows(place, part_ref, mine_ref, theirs_ref)


def ring_sum(recv, rows):
    total = recv[0, rows, :].astype(F32)
    for index in range(1, RING):
        total = total + recv[index, rows, :].astype(F32)
    return total


def in_grads_kernel(
    place, tokens, d, d_pair, pair_in, ob, low, low_pair, sums, unit_sums, out_ref
):
    shard = place[0]
    rows = jnp.concatenate([tokens[:, half_at(shard, True)], pair_in[:, 256:768]], axis=0)
    grads = jnp.concatenate([d[...], d_pair[...]], axis=0)
    for part in range(3):
        term = mm(rows, grads[:, part * COLS : (part + 1) * COLS], TN).astype(BF)
        out_ref[:, part * 32 : part * 32 + 32, :] = term.reshape(RING, 32, COLS)
    heads = jnp.concatenate([ob[...], pair_in[:, 0:256]], axis=0)
    outs = jnp.concatenate([low[...], low_pair[...]], axis=0)
    for side in range(2):
        term = mm(heads, outs[:, side * COLS : (side + 1) * COLS], TN).astype(BF)
        out_ref[:, 96 + side * 16 : 112 + side * 16, :] = term.reshape(RING, 16, COLS)
    wide = grads.astype(F32)
    small = jnp.concatenate(
        [
            sums[0:6, :],
            jnp.sum(wide[:, 0:COLS], axis=0, keepdims=True),
            jnp.sum(wide[:, 2 * COLS : 3 * COLS], axis=0, keepdims=True),
            unit_sums[...],
        ],
        axis=0,
    ).astype(BF)
    for index in range(RING):
        out_ref[index, 128:144, :] = small


def unit_total_kernel(place, recv, low_ref):
    low_ref[...] = ring_sum(recv, slice(0, 256)).astype(BF)


def total_kernel(place, recv, small_ref, out_ref):
    total = ring_sum(recv, slice(0, 144))
    small_ref[...] = total[128:144]
    low = total[0:128].astype(BF)
    for index in range(RING):
        out_ref[index] = low


def unpack_units_kernel(place, recv, up_ref, down_ref):
    for part in range(4):
        up_ref[:, part * COLS : (part + 1) * COLS] = (
            recv[:, part * 32 : part * 32 + 32, :].reshape(HALF, COLS).astype(F32)
        )
    for side in range(2):
        down_ref[:, side * COLS : (side + 1) * COLS] = (
            recv[:, 128 + side * 64 : 192 + side * 64, :].reshape(UNITS, COLS).astype(F32)
        )


def unpack_kernel(place, recv, in_ref, out_ref):
    for part in range(3):
        in_ref[part] = recv[:, part * 32 : part * 32 + 32, :].reshape(HALF, COLS).astype(F32)
    for side in range(2):
        out_ref[:, side * COLS : (side + 1) * COLS] = (
            recv[:, 96 + side * 16 : 112 + side * 16, :].reshape(COLS, COLS).astype(F32)
        )


def swap(value, axis, bit):
    size = lax.axis_size(axis)
    return lax.ppermute(value, axis, [(index, index ^ bit) for index in range(size)])


def tensor_sum(mine, theirs):
    chip = (mine.astype(F32) + swap(theirs, "tensor", 1).astype(F32)).astype(BF)
    return chip, swap(chip, "tensor", 2)


def shards(
    tokens, segment_ids, w_qkv, b_qv, w_out, w_up, b_up, w_down, out_bias, ln_gain, ln_bias, cotangent
):
    shard, block, tensor = (lax.axis_index(name) for name in ("shard", "context", "tensor"))
    core, far = tensor % 2, tensor // 2
    place = jnp.stack([shard, block, core, far]).astype(jnp.int32)
    w_in = jnp.transpose(w_qkv[0], (1, 0, 2))
    w_out, w_up, w_down = w_out[0], w_up[0], w_down[0]
    extra, gain, shift = out_bias[0], ln_gain[0], ln_bias[0]
    together = lax.optimization_barrier

    up_rows = lax.dynamic_slice_in_dim(w_up, block * 32, 32, 0)
    down_rows = lax.dynamic_slice_in_dim(w_down, block * 64, 64, 0)
    unit_rows = swap(
        jnp.concatenate([up_rows[:, :HALF], up_rows[:, HALF:], down_rows], axis=0), "shard", 1
    )
    other = lax.all_gather(unit_rows, "context", axis=0)
    w_in_late, _ = together((w_in, unit_rows))
    in_oth = swap(w_in_late, "shard", 1)
    out_oth = swap(w_out, "shard", 1)

    spread = jnp.broadcast_to(
        jnp.where(core == 0, tokens[0:64], tokens[64:128])[None], (RING, 64, D)
    )
    x_mine = lax.all_to_all(spread, "context", 0, 0, tiled=True)
    x_mine, in_oth, out_oth = together((x_mine, in_oth, out_oth))
    x_sib = swap(x_mine, "tensor", 1)

    id_column = segment_ids.reshape(RING, BLK, 1)
    id_heads = jnp.tile(segment_ids.reshape(RING, 1, BLK), (1, 1, HEADS))
    all_heads = ((RING, 2, 64, COLS), BF)
    halves = [((64, D), BF), ((64, D), BF)]
    whole = pltpu.VMEM((BLK, D), F32)
    q, k, v, o, ob, lse, mine, theirs = call(
        attend_kernel, 10,
        [((BLK, COLS), BF)] + [all_heads] * 2 + [((BLK, COLS), F32), ((BLK, COLS), BF), ((1, HEADS * BLK), F32)] + halves,
        place, x_mine, x_sib, tokens, w_in, in_oth, b_qv[0], id_heads, id_column,
        w_out, out_oth,
        scratch=[whole], vmem=60,
    )
    chip, recv = tensor_sum(mine, theirs)
    first, low_mid = call(
        first_norm_kernel, 1, [((64, D), F32), ((64, D), BF)],
        place, tokens, chip, recv, extra, gain, shift,
    )
    hb_sib = swap(low_mid, "tensor", 1)
    ub, slope, mine, theirs = call(
        up_down_kernel, 2, [((BLK, UNITS), BF), ((BLK, UNITS), F32)] + halves,
        place, low_mid, hb_sib, w_up, w_down, other, b_up,
        scratch=[whole],
    )
    away = (1 - shard) * HALF

    def away_half(mine, sibling):
        rows = [lax.dynamic_slice_in_dim(half, away, HALF, 1) for half in (mine, sibling)]
        return jnp.concatenate(rows, axis=0)

    pair_in = swap(
        jnp.concatenate([ob, lax.dynamic_slice_in_dim(tokens, away, HALF, 1)], axis=1), "shard", 1
    )
    pair_ub = swap(ub[:, 0:EARLY], "shard", 1)
    chip, recv = tensor_sum(mine, theirs)
    hidden_out, dx, low_second, sums = call(
        second_norm_kernel, 2,
        [((32, D), F32), ((BLK, D), F32), ((64, D), BF), ((8, D), F32)],
        place, first, chip, recv, extra, gain, shift, cotangent,
        scratch=[pltpu.VMEM((64, D), F32)],
    )
    dz_sib = swap(low_second, "tensor", 1)
    dz_sib, pair_ub = together((dz_sib, pair_ub))
    pair_dz = swap(away_half(low_second, dz_sib), "shard", 1)
    da, mine, theirs = call(
        down_up_kernel, 2, [((BLK, UNITS), BF)] + halves,
        place, low_second, dz_sib, slope, w_up, w_down, other,
        scratch=[whole],
    )
    pair_da = swap(da, "shard", 1)
    chip, recv = tensor_sum(mine, theirs)
    d_first, low_first, sums = call(
        first_back_kernel, 1.5,
        [((32, D), F32), ((64, D), BF), ((8, D), F32)],
        place, dx, chip, recv, gain, shift, sums,
        scratch=[pltpu.VMEM((64, D), F32)],
    )
    low_sib = swap(low_first, "tensor", 1)
    low_own, low_oth, d_out, delta, packed = call(
        out_back_kernel, 1.5,
        [
            ((BLK, HALF), BF), ((BLK, HALF), BF), ((BLK, COLS), BF), ((1, HEADS * BLK), F32),
            ((RING, 144, COLS), BF),
        ],
        place, low_first, low_sib, o, lse, w_out, out_oth,
        scratch=[pltpu.VMEM((BLK, D), BF)], vmem=60,
    )
    ub, packed = together((ub, packed))
    packs = lax.all_to_all(packed, "context", 0, 0, tiled=True)
    pair_late = swap(
        jnp.concatenate([away_half(low_mid, hb_sib), ub[:, EARLY:UNITS]], axis=1), "shard", 1
    )
    (dq,) = call(
        query_grad_kernel, 5, [((BLK, COLS), BF)],
        place, q, k, v, d_out, lse, delta, id_heads, id_column,
        scratch=[pltpu.VMEM((HEADS * BLK, COLS), F32)], vmem=60,
    )
    low_mid, dq = together((low_mid, dq))
    unit_grads, unit_small = call(
        unit_grads_kernel, 3, [((RING, 256, COLS), BF), ((8, COLS), F32)],
        place, low_mid, hb_sib, da, ub, low_second, dz_sib, pair_ub, pair_late, pair_dz, pair_da,
    )
    packs, unit_grads, dq = together((packs, unit_grads, dq))
    unit_recv = lax.all_to_all(unit_grads, "context", 0, 0, tiled=True)
    low_pair = swap(low_oth, "shard", 1)
    sums = sums + swap(sums, "tensor", 1)
    sums = lax.dynamic_slice_in_dim(sums, tensor * COLS, COLS, 1)
    sums = sums + swap(sums, "shard", 1)
    d_mixed, mine, theirs = call(
        key_grad_kernel, 6, [((BLK, 3 * COLS), BF)] + halves,
        place, x_mine, x_sib, b_qv[0], k, v, dq, packs, id_heads, id_column, w_in, in_oth,
        scratch=[whole, pltpu.VMEM((RING, 2, 64, COLS), BF)], vmem=60,
    )
    d_pair = swap(d_mixed, "shard", 1)
    chip = mine.astype(F32) + swap(theirs, "tensor", 1).astype(F32)
    chip_far = lax.dynamic_slice_in_dim(chip, (1 - far) * 32, 32, 0).astype(BF)
    chip_near = lax.dynamic_slice_in_dim(chip, far * 32, 32, 0)
    grad_tokens = d_first + (chip_near + swap(chip_far, "tensor", 2).astype(F32))
    (in_grads,) = call(
        in_grads_kernel, 2.5, [((RING, 144, COLS), BF)],
        place, tokens, d_mixed, d_pair, pair_in, ob, low_own, low_pair, sums, unit_small,
    )
    in_grads, unit_recv = together((in_grads, unit_recv))
    recv = lax.all_to_all(in_grads, "context", 0, 0, tiled=True)
    (unit_total,) = call(unit_total_kernel, 1, [((COLS, COLS), BF)], place, unit_recv)
    unit_all = lax.all_gather(unit_total, "context", axis=0)
    recv, _ = together((recv, unit_total))
    small, totals = call(
        total_kernel, 2, [((16, COLS), F32), ((RING, 128, COLS), BF)], place, recv
    )
    recv = lax.all_to_all(totals, "context", 0, 0, tiled=True)
    grad_in, grad_w_out = call(
        unpack_kernel, 2, [((3, HALF, COLS), F32), ((COLS, HALF), F32)], place, recv
    )
    grad_w_up, grad_w_down = call(
        unpack_units_kernel, 2, [((HALF, UNITS), F32), ((UNITS, HALF), F32)],
        place, unit_all, vmem=60,
    )
    return (
        hidden_out,
        grad_tokens,
        jnp.transpose(grad_in, (1, 0, 2))[None],
        grad_w_out[None],
        grad_w_up[None],
        grad_w_down[None],
        small[6:8][None],
        small[8:12].reshape(1, UNITS),
        jnp.stack([small[3], small[0]])[None],
        jnp.stack([small[4], small[1]])[None],
        jnp.stack([small[5], small[2]])[None],
    )


def solution(mesh):
    rows = P(("shard", "context"), None)
    own_rows = P(("shard", "context", "tensor"), None)
    by_column = P(None, None, "tensor")
    in_specs = (
        rows,
        P("shard"),
        P(None, "shard", None, "tensor"),
        by_column,
        P(None, "tensor", "shard"),
        P(None, "shard", "tensor"),
        P(None, "tensor"),
        P(None, "tensor", "shard"),
        P(),
        P(),
        P(),
        rows,
    )
    out_specs = (
        own_rows,
        own_rows,
        P(None, "shard", None, "tensor"),
        P(None, "tensor", "shard"),
        P(None, "shard", "tensor"),
        P(None, "tensor", "shard"),
        by_column,
        P(None, "tensor"),
        by_column,
        by_column,
        by_column,
    )
    return jax.shard_map(shards, mesh=mesh, in_specs=in_specs, out_specs=out_specs, check_vma=False)
```
